256 devices in a mesh: segment: 4 (over x), seq: 64 (over z, y, core).
Axes of the slice: x: 4, y: 4, z: 8, core: 2. Of those that a mesh axis runs over, the one named last changes fastest.
Arguments:
- layer_inputs: bfloat16 [4, 65536, 512], P('segment', 'seq'), may hold values from -6 to 6
- first_blocks: bfloat16 [4, 256, 256, 256], P('segment', 'seq'), may hold values from -0.375 to 0.375
- second_blocks: bfloat16 [4, 256, 256, 256], P('segment', 'seq'), may hold values from -0.375 to 0.375
- gate_scale: float32 [4, 512], P('segment'), may hold values from -4 to 4
- gate_shift: float32 [4, 512], P('segment'), may hold values from -4 to 4
- top_grads: bfloat16 [65536, 512], P('seq'), may hold values from -1.5 to 1.5
Outputs:
- input_grads: bfloat16 [4, 65536, 512], P('segment', 'seq')
- second_grads: float32 [4, 256, 256, 256], P('segment', 'seq')
The draws below stay inside these ranges and needn't reach their ends.
All inputs are finite; a program needn't handle non-finite values.
Results may differ from the reference program's by a relative error of at most 0.015.
Values may be sent and summed in bfloat16 or wider, within the bound.
No kernel may reach another device: no remote copies, remote signals or barrier semaphores. Data moves between devices by JAX's collectives and lax.ppermute only.
A program may use at most 64 MiB of HBM per device.

```python
import jax
import jax.numpy as jnp

D = 512
BLOCK = 256
ROWS = 256
TOKENS = 65536
N_SEGMENT = 4


def steps_of(own_key, dims, pieces, least, largest):
    def one(dim, blocks):
        heights = jax.random.uniform(jax.random.fold_in(jax.random.fold_in(own_key, 6), dim), (blocks,), jnp.float32, least / len(pieces), largest / len(pieces))
        return jnp.repeat(jnp.exp(heights), dims[dim] // blocks).reshape((-1,) + (1,) * (len(dims) - dim - 1))

    level = one(*pieces[0])
    for cut in pieces[1:]:
        level = level * one(*cut)
    return level


def scatter_about(rng, dims, spread, reach, shards=(), kind=jnp.bfloat16):
    entries = jax.random.normal(rng, dims, jnp.float32) * spread
    if len(shards) > 0:
        entries = steps_of(rng, dims, shards, -0.22, 0.18) * entries
    return jnp.clip(entries, min=-reach, max=reach).astype(kind)


def setup_inputs(seed: int = 0) -> dict:
    seeds = jax.random.split(jax.random.key(seed), 7)
    layer_inputs = scatter_about(seeds[0], (N_SEGMENT, TOKENS, D), 1.0, 6.0, ((0, 4), (1, 64)))
    first_blocks = scatter_about(seeds[1], (N_SEGMENT, ROWS, BLOCK, BLOCK), BLOCK ** -0.5, 0.375, ((0, 4), (1, 64)))
    second_blocks = scatter_about(seeds[2], (N_SEGMENT, BLOCK, ROWS, ROWS), ROWS ** -0.5, 0.375, ((0, 4), (1, 64)))
    gate_scale = scatter_about(seeds[3], (N_SEGMENT, D), 1.0, 4.0, ((0, 4),), jnp.float32)
    gate_shift = scatter_about(seeds[4], (N_SEGMENT, D), 1.0, 4.0, ((0, 4),), jnp.float32)
    top_grads = scatter_about(seeds[5], (TOKENS, D), 0.25, 1.5, ((0, 64),))
    return dict(layer_inputs=layer_inputs, first_blocks=first_blocks, second_blocks=second_blocks, gate_scale=gate_scale, gate_shift=gate_shift, top_grads=top_grads)


def layer_backward(inputs, firsts, seconds, scale, shift, upstream):
    rows = firsts.shape[0]
    block = firsts.shape[1]
    width = inputs.shape[1]
    inputs3 = inputs.reshape(rows, block, width).astype(jnp.float32)
    upstream3 = upstream.reshape(rows, block, width).astype(jnp.float32)
    firsts32 = firsts.astype(jnp.float32)
    seconds32 = seconds.astype(jnp.float32)
    gate_value = jax.nn.sigmoid(inputs3 * scale + shift)
    first_mixed = jnp.einsum('rpc,rcd->rpd', firsts32, inputs3).astype(jnp.bfloat16)
    mixed = jnp.einsum('pqr,rpd->qpd', seconds32, first_mixed.astype(jnp.float32)).astype(jnp.bfloat16)
    grad_mixed = (upstream3 * gate_value).astype(jnp.bfloat16)
    gate_slope = (upstream3 * gate_value * (1.0 - gate_value)).astype(jnp.bfloat16)
    gate_grad = (gate_slope.astype(jnp.float32) * mixed.astype(jnp.float32)).astype(jnp.bfloat16)
    back_first = jnp.einsum('pqr,qpd->rpd', seconds32, grad_mixed.astype(jnp.float32)).astype(jnp.bfloat16)
    second_grad = jnp.einsum('qpd,rpd->pqr', grad_mixed.astype(jnp.float32), first_mixed.astype(jnp.float32))
    through = jnp.einsum('rpc,rpd->rcd', firsts32, back_first.astype(jnp.float32))
    result = upstream3 + through + gate_grad.astype(jnp.float32) * scale
    return result.astype(jnp.bfloat16).reshape(rows * block, width), second_grad


def reference(layer_inputs, first_blocks, second_blocks, gate_scale, gate_shift, top_grads):
    segments = layer_inputs.shape[0]
    upstream = top_grads
    grads_list = [None] * segments
    second_list = [None] * segments
    for level in range(segments - 1, -1, -1):
        grads_here, second_here = layer_backward(layer_inputs[level], first_blocks[level], second_blocks[level], gate_scale[level], gate_shift[level], upstream)
        grads_list[level] = grads_here
        second_list[level] = second_here
        upstream = grads_here
    return jnp.stack(grads_list), jnp.stack(second_list)
```

```python
import functools

import jax
import jax.numpy as jnp
from jax import lax
from jax.experimental import pallas as pl
from jax.experimental.pallas import tpu as pltpu
from jax.sharding import PartitionSpec as P

BF = jnp.bfloat16
F32 = jnp.float32
VMEM_LIMIT = 16 * 1024 * 1024


def dot(a, b):
    return lax.dot_general(a, b, (((1,), (0,)), ((), ())), preferred_element_type=F32)


def dot_first(a, b):
    return lax.dot_general(a, b, (((0,), (0,)), ((), ())), preferred_element_type=F32)


def dot_last(a, b):
    return lax.dot_general(a, b, (((1,), (1,)), ((), ())), preferred_element_type=F32)


def spread(block, chunks, row):
    for col in range(4):
        chunks[pl.ds(row * 4 + col, 64, stride=16), :] = block[pl.ds(col, 64, stride=4), :]


def collect(chunks, block, row):
    for col in range(4):
        block[pl.ds(col, 64, stride=4), :] = chunks[pl.ds(row * 4 + col, 64, stride=16), :]


def first_kernel(firsts, inputs, out, block, chunks):
    for part in range(4):
        for row in range(4):
            block[...] = dot(firsts[row], inputs[row, :, part * 128:(part + 1) * 128])
            spread(block, chunks, row)
        out[part * 1024:(part + 1) * 1024, :] = chunks[...].astype(BF)


def gate_kernel(plane, upstream, own, near, far, last, own_v, near_v, far_v, last_v, out, held, vectors, block, chunks):
    index = plane[0]
    for step, (part, vector) in enumerate(((own, own_v), (near, near_v), (far, far_v), (last, last_v))):
        layer = (index + 4 - step) % 4
        held[layer] = part[...]
        vectors[layer] = vector[...]
    for row in range(4):
        rows = slice(row * 256, (row + 1) * 256)
        gate = jax.nn.sigmoid(held[3, rows, :].astype(F32) * vectors[3, 0:1, :] + vectors[3, 1:2, :])
        block[...] = upstream[rows, :].astype(F32) * gate
        spread(block, chunks, row)
    out[...] = chunks[...].astype(BF)


def column_kernel(layer, seconds, grads, firsts_out, out, wide_grads, wide_firsts, back, mixed):
    wide_grads[...] = grads[...].astype(F32)
    wide_firsts[...] = firsts_out[layer * 1024:(layer + 1) * 1024, :].astype(F32)
    for col in range(4):
        rows = pl.ds(col, 256, stride=4)
        weight = seconds[layer, col]
        back[rows, :] = dot_first(weight, wide_grads[rows, :].astype(BF))
        mixed[rows, :] = dot(weight, wide_firsts[rows, :].astype(BF))
    out[:, :16, :] = back[...].astype(BF).reshape(64, 16, 128)
    out[:, 16:, :] = mixed[...].astype(BF).reshape(64, 16, 128)


def second_kernel(grads0, grads1, grads2, grads3, firsts_out, out, wide_grads, wide_firsts):
    for layer, grads in enumerate((grads0, grads1, grads2, grads3)):
        wide_grads[...] = grads[...].astype(F32)
        wide_firsts[...] = firsts_out[layer * 1024:(layer + 1) * 1024, :].astype(F32)
        for col in range(4):
            rows = pl.ds(col, 256, stride=4)
            out[layer, col] = dot_last(
                wide_grads[rows, :].astype(BF), wide_firsts[rows, :].astype(BF)
            ).astype(BF)


def row_kernel(layer, received, firsts, upstream, held, vectors, *rest):
    last = layer == 0
    if last:
        out, chunks, mixed_chunks, block, mixed_block = rest
    else:
        out, next_out, chunks, mixed_chunks, block, mixed_block, next_chunks = rest
    chunks[...] = received[:, :16, :].reshape(1024, 128).astype(F32)
    mixed_chunks[...] = received[:, 16:, :].reshape(1024, 128).astype(F32)
    scale, shift = vectors[layer, 0:1, :], vectors[layer, 1:2, :]
    for row in range(4):
        rows = slice(row * 256, (row + 1) * 256)
        collect(chunks, block, row)
        collect(mixed_chunks, mixed_block, row)
        through = dot_first(firsts[layer, row], block[...].astype(BF))
        up = upstream[rows, :].astype(F32)
        gate = jax.nn.sigmoid(held[layer, rows, :].astype(F32) * scale + shift)
        slope = (up * gate * (1.0 - gate)).astype(BF).astype(F32)
        gate_grad = (slope * mixed_block[...]).astype(BF).astype(F32)
        result = (up + through + gate_grad * scale).astype(BF)
        out[rows, :] = result
        if not last:
            after = layer - 1
            gate = jax.nn.sigmoid(
                held[after, rows, :].astype(F32) * vectors[after, 0:1, :] + vectors[after, 1:2, :]
            )
            block[...] = result.astype(F32) * gate
            spread(block, next_chunks, row)
    if not last:
        next_out[...] = next_chunks[...].astype(BF)


def final_kernel(own, near, far, last, out):
    for part, value in enumerate((own, near, far, last)):
        out[:, part * 128:(part + 1) * 128] = value[...]


IN_VMEM = pl.BlockSpec(memory_space=pltpu.VMEM)
IN_SMEM = pl.BlockSpec(memory_space=pltpu.SMEM)


def call(kernel, count, out_shapes, scratch, flops, scalars=0):
    outs = [jax.ShapeDtypeStruct(s, d) for s, d in out_shapes]
    single = len(outs) == 1
    return pl.pallas_call(
        kernel,
        in_specs=[IN_SMEM] * scalars + [IN_VMEM] * count,
        out_shape=outs[0] if single else outs,
        out_specs=IN_VMEM if single else [IN_VMEM] * len(outs),
        scratch_shapes=[pltpu.VMEM(s, F32) for s in scratch],
        compiler_params=pltpu.CompilerParams(vmem_limit_bytes=VMEM_LIMIT),
        cost_estimate=pl.CostEstimate(flops=flops, bytes_accessed=2 << 20, transcendentals=0),
    )


TALL = (1024, 128)
BLOCK = (256, 128)
FLOPS = 2 * 4 * 256 * 256 * 128


def body(layer_inputs, first_blocks, second_blocks, gate_scale, gate_shift, top_grads):
    plane = lax.axis_index("segment")
    index = plane.astype(jnp.int32).reshape(1)
    inputs = layer_inputs[0]
    vectors = jnp.concatenate([gate_scale, gate_shift], 0)

    seconds_all = lax.all_gather(second_blocks, "segment", tiled=True)
    firsts_all = lax.all_gather(first_blocks, "segment", tiled=True)

    parts, own_vectors = [], []
    for step in range(4):
        start = ((plane + step) % 4) * 128
        part = lax.dynamic_slice_in_dim(inputs, start, 128, 1)
        vector = lax.dynamic_slice_in_dim(vectors, start, 128, 1)
        if step > 0:
            ring = [(i, (i + step) % 4) for i in range(4)]
            part = lax.ppermute(part, "segment", ring)
            vector = lax.ppermute(vector, "segment", ring)
        parts.append(part)
        own_vectors.append(vector)

    firsts_out = call(first_kernel, 2, [((4096, 128), BF)], [BLOCK, TALL], 4 * FLOPS)(
        first_blocks[0], inputs.reshape(4, 256, 512)
    )
    firsts_cols = lax.all_to_all(
        firsts_out.reshape(256, 16, 128), ("segment", "seq"), 0, 0, tiled=True
    ).reshape(4096, 128)

    upstream = lax.dynamic_slice_in_dim(top_grads, plane * 128, 128, 1)
    sends, held, vectors = call(
        gate_kernel,
        9,
        [(TALL, BF), ((4, 1024, 128), BF), ((4, 2, 128), F32)],
        [BLOCK, TALL],
        1 << 20,
        scalars=1,
    )(index, upstream, *parts, *own_vectors)

    results, grads = [None] * 4, [None] * 4
    for l in (3, 2, 1, 0):
        grads[l] = lax.all_to_all(sends.reshape(64, 16, 128), "seq", 0, 0, tiled=True).reshape(TALL)
        payload = call(
            functools.partial(column_kernel, l), 3, [((64, 32, 128), BF)], [TALL] * 4, 2 * FLOPS
        )(seconds_all, grads[l], firsts_cols)
        received = lax.all_to_all(payload, "seq", 0, 0, tiled=True)
        outs, scratch = [(TALL, BF)], [TALL, TALL, BLOCK, BLOCK]
        if l > 0:
            outs, scratch = outs + [(TALL, BF)], scratch + [TALL]
        made = call(functools.partial(row_kernel, l), 5, outs, scratch, FLOPS)(
            received, firsts_all, upstream, held, vectors
        )
        upstream, sends = (made, None) if l == 0 else made
        results[l] = upstream

    partials = call(second_kernel, 5, [((4, 4, 256, 256), BF)], [TALL, TALL], 4 * FLOPS)(
        *grads, firsts_cols
    )
    second = lax.psum_scatter(partials, "segment", scatter_dimension=0, tiled=True)
    back = lax.all_to_all(jnp.stack(results), "segment", 0, 0, tiled=True)
    grads_out = call(final_kernel, 4, [((1024, 512), BF)], [], 1 << 20)(*[back[i] for i in range(4)])
    return grads_out[None], second.astype(F32)


def solution(mesh):
    placed = (
        P("segment", "seq", None),
        P("segment", "seq", None, None),
        P("segment", "seq", None, None),
        P("segment", None),
        P("segment", None),
        P("seq", None),
    )
    return jax.shard_map(
        body,
        mesh=mesh,
        in_specs=placed,
        out_specs=(P("segment", "seq", None), P("segment", "seq", None, None)),
        check_vma=False,
    )
```

```python
import functools

import jax
import jax.numpy as jnp
from jax import lax
from jax.experimental import pallas as pl
from jax.experimental.pallas import tpu as pltpu
from jax.sharding import PartitionSpec as P

BF = jnp.bfloat16
F32 = jnp.float32
VMEM_LIMIT = 6 * 1024 * 1024
LARGE_LIMIT = 58 * 1024 * 1024


def dot(a, b):
    return lax.dot_general(a, b, (((1,), (0,)), ((), ())), preferred_element_type=F32)


def dot_first(a, b):
    return lax.dot_general(a, b, (((0,), (0,)), ((), ())), preferred_element_type=F32)


def dot_last(a, b):
    return lax.dot_general(a, b, (((1,), (1,)), ((), ())), preferred_element_type=F32)


def spread(block, chunks, row):
    for col in range(4):
        chunks[pl.ds(row * 4 + col, 64, stride=16), :] = block[pl.ds(col, 64, stride=4), :]


def collect(chunks, block, row):
    for col in range(4):
        block[pl.ds(col, 64, stride=4), :] = chunks[pl.ds(row * 4 + col, 64, stride=16), :]


def first_kernel(firsts, inputs, scale, shift, tops, out, upstream, block, chunks, vectors, both, weights, held, sems):
    lanes = pl.ds(pl.multiple_of(lax.axis_index("segment") * 128, 128), 128)
    copies = []
    for row in range(4):
        copies.append(pltpu.make_async_copy(firsts.at[row], weights.at[row], sems.at[2 * row]))
        copies.append(pltpu.make_async_copy(inputs.at[row], held.at[row], sems.at[2 * row + 1]))
    copies.append(pltpu.make_async_copy(scale, both.at[0:1, :], sems.at[8]))
    copies.append(pltpu.make_async_copy(shift, both.at[1:2, :], sems.at[9]))
    copies.append(pltpu.make_async_copy(tops.at[:, lanes], upstream, sems.at[10]))
    for copy in copies:
        copy.start()
    for copy in copies:
        copy.wait()
    vectors[...] = jnp.zeros_like(vectors)
    for part in range(4):
        lanes = slice(part * 128, (part + 1) * 128)
        for row in range(4):
            out[part, row * 256:(row + 1) * 256, :] = held[row, :, lanes]
            block[...] = dot(weights[row], held[row, :, lanes])
            spread(block, chunks, row)
        out[part, 1024:2048, :] = chunks[...].astype(BF)
        for place in range(2):
            left = both[place:place + 1, lanes]
            for term in range(3):
                piece = left.astype(BF).astype(F32)
                vectors[place * 3 + term:place * 3 + term + 1, :] = piece
                left = left - piece
        out[part, 2048:, :] = vectors[...].astype(BF)


def gated(held, vectors, layer, rows):
    scale, shift = vectors[layer, 0:1, :], vectors[layer, 1:2, :]
    return jax.nn.sigmoid(held[layer, rows, :].astype(F32) * scale + shift), scale


def gate_kernel(upstream, held, out, vectors, block, chunks):
    for layer in range(4):
        terms = held[layer, 2048:, :].astype(F32)
        vectors[layer, 0:1, :] = terms[0:1, :] + (terms[1:2, :] + terms[2:3, :])
        vectors[layer, 1:2, :] = terms[3:4, :] + (terms[4:5, :] + terms[5:6, :])
    for row in range(4):
        rows = slice(row * 256, (row + 1) * 256)
        gate, _ = gated(held, vectors, 3, rows)
        block[...] = upstream[rows, :].astype(F32) * gate
        spread(block, chunks, row)
    out[:, 0] = chunks[...].astype(BF).reshape(64, 16, 128)
    for place, layer in ((1, 3), (2, 2), (3, 1)):
        out[:, place] = held[layer, 1024:2048, :].reshape(64, 16, 128)


def column_kernel(layer, seconds, received, out, wide, result):
    for place, owner in enumerate(MIXED[layer]):
        wide[...] = received[:, place].reshape(1024, 128).astype(F32)
        for col in range(4):
            rows = pl.ds(col, 256, stride=4)
            times = dot_first if place == 0 else dot
            result[rows, :] = times(seconds[owner, col], wide[rows, :].astype(BF))
        out[:, place] = result[...].astype(BF).reshape(64, 16, 128)


def second_kernel(zero, one, two, three, out, grads, firsts_out):
    firsts = ((zero, 1), (three, 3), (three, 2), (three, 1))
    for layer, received in enumerate((zero, one, two, three)):
        source, place = firsts[layer]
        grads[...] = received[:, 0].reshape(1024, 128).astype(F32)
        firsts_out[...] = source[:, place].reshape(1024, 128).astype(F32)
        for col in range(4):
            rows = pl.ds(col, 256, stride=4)
            out[layer, col] = dot_last(
                grads[rows, :].astype(BF), firsts_out[rows, :].astype(BF)
            ).astype(BF)


def row_kernel(layer, received, mixed, firsts, upstream, held, vectors, *rest):
    if layer == 0:
        out, chunks, mixed_chunks, block, mixed_block = rest
    else:
        out, next_out, chunks, mixed_chunks, block, mixed_block, next_chunks = rest
    place = (1, 3, 2, 1)[layer]
    chunks[...] = received[:, 0].reshape(1024, 128).astype(F32)
    mixed_chunks[...] = mixed[:, place].reshape(1024, 128).astype(F32)
    for row in range(4):
        rows = slice(row * 256, (row + 1) * 256)
        collect(chunks, block, row)
        collect(mixed_chunks, mixed_block, row)
        through = dot_first(firsts[layer, row], block[...].astype(BF))
        up = upstream[rows, :].astype(F32)
        gate, scale = gated(held, vectors, layer, rows)
        slope = (up * gate * (1.0 - gate)).astype(BF).astype(F32)
        gate_grad = (slope * mixed_block[...]).astype(BF).astype(F32)
        result = (up + through + gate_grad * scale).astype(BF)
        out[rows, :] = result
        if layer > 0:
            gate, _ = gated(held, vectors, layer - 1, rows)
            block[...] = result.astype(F32) * gate
            spread(block, next_chunks, row)
    if layer > 0:
        next_out[:, 0] = next_chunks[...].astype(BF).reshape(64, 16, 128)
        if layer == 1:
            next_out[:, 1] = held[0, 1024:2048, :].reshape(64, 16, 128)


def end_kernel(zero, one, two, three, *outs):
    index = lax.axis_index("segment")
    for step, out in enumerate(outs):
        for layer, value in enumerate((zero, one, two, three)):
            @pl.when((index + step) % 4 == layer)
            def _():
                out[...] = value[...]


def final_kernel(own, near, far, last, out):
    index = lax.axis_index("segment")
    for step, value in enumerate((own, near, far, last)):
        lanes = pl.ds(pl.multiple_of(((index + 4 - step) % 4) * 128, 128), 128)
        out[:, lanes] = value[...]


IN_VMEM = pl.BlockSpec(memory_space=pltpu.VMEM)


IN_HBM = pl.BlockSpec(memory_space=pltpu.HBM)


def call(kernel, count, out_shapes, scratch, flops, fetched=0, copies=0, grant=VMEM_LIMIT):
    outs = [jax.ShapeDtypeStruct(s, d) for s, d in out_shapes]
    single = len(outs) == 1
    return pl.pallas_call(
        kernel,
        in_specs=[IN_VMEM] * (count - fetched) + [IN_HBM] * fetched,
        out_shape=outs[0] if single else outs,
        out_specs=IN_VMEM if single else [IN_VMEM] * len(outs),
        scratch_shapes=[pltpu.VMEM(*s) if isinstance(s[0], tuple) else pltpu.VMEM(s, F32) for s in scratch]
        + ([pltpu.SemaphoreType.DMA((copies,))] if copies else []),
        compiler_params=pltpu.CompilerParams(vmem_limit_bytes=grant),
        cost_estimate=pl.CostEstimate(flops=flops, bytes_accessed=2 << 20, transcendentals=0),
    )


TALL = (1024, 128)
MIXED = {3: (3, 3, 2, 1), 2: (2,), 1: (1,), 0: (0, 0)}
BLOCK = (256, 128)
FLOPS = 2 * 4 * 256 * 256 * 128


def body(layer_inputs, first_blocks, second_blocks, gate_scale, gate_shift, top_grads):
    payload, upstream = call(
        first_kernel,
        5,
        [((4, 2064, 128), BF), (TALL, BF)],
        [BLOCK, TALL, (16, 128), (2, 512), ((4, 256, 256), BF), ((4, 256, 512), BF)],
        4 * FLOPS,
        fetched=5,
        copies=11,
        grant=LARGE_LIMIT,
    )(first_blocks[0], layer_inputs[0].reshape(4, 256, 512), gate_scale, gate_shift, top_grads)
    held = lax.all_to_all(payload, "segment", 0, 0, tiled=True)
    held, first_blocks, second_blocks = lax.optimization_barrier((held, first_blocks, second_blocks))
    seconds_all = lax.all_gather(second_blocks, "segment", tiled=True)
    firsts_all = lax.all_gather(first_blocks, "segment", tiled=True)
    sends, vectors = call(
        gate_kernel, 2, [((64, 4, 16, 128), BF), ((4, 2, 128), F32)], [BLOCK, TALL], 1 << 20
    )(upstream, held)

    results, columns = [None] * 4, [None] * 4
    for l in (3, 2, 1, 0):
        places = len(MIXED[l])
        columns[l] = lax.all_to_all(sends, "seq", 0, 0, tiled=True)
        payload = call(
            functools.partial(column_kernel, l),
            2,
            [((64, places, 16, 128), BF)],
            [TALL] * 2,
            places * FLOPS,
        )(seconds_all, columns[l])
        if l == 0:
            partials = call(
                second_kernel, 4, [((4, 4, 256, 256), BF)], [TALL, TALL], 4 * FLOPS
            )(*columns)
            payload, partials = lax.optimization_barrier((payload, partials))
        received = lax.all_to_all(payload, "seq", 0, 0, tiled=True)
        if places > 1:
            mixed = received
        outs, scratch = [(TALL, BF)], [TALL, TALL, BLOCK, BLOCK]
        if l > 0:
            outs, scratch = outs + [((64, len(MIXED[l - 1]), 16, 128), BF)], scratch + [TALL]
        made = call(functools.partial(row_kernel, l), 6, outs, scratch, FLOPS)(
            received, mixed, firsts_all, upstream, held, vectors
        )
        upstream, sends = (made, None) if l == 0 else made
        results[l] = upstream

    second = lax.psum_scatter(partials, "segment", scatter_dimension=0, tiled=True).astype(F32)
    back = list(call(end_kernel, 4, [(TALL, BF)] * 4, [], 1 << 20)(*results))
    for step in (1, 2, 3):
        back[step] = lax.ppermute(back[step], "segment", [(i, (i + step) % 4) for i in range(4)])
    back, second = lax.optimization_barrier((back, second))
    grads_out = call(final_kernel, 4, [((1024, 512), BF)], [], 1 << 20)(*back)
    return grads_out[None], second


def solution(mesh):
    placed = (
        P("segment", "seq", None),
        P("segment", "seq", None, None),
        P("segment", "seq", None, None),
        P("segment", None),
        P("segment", None),
        P("seq", None),
    )
    return jax.shard_map(
        body,
        mesh=mesh,
        in_specs=placed,
        out_specs=(P("segment", "seq", None), P("segment", "seq", None, None)),
        check_vma=False,
    )
```

```python
import functools

import jax
import jax.numpy as jnp
from jax import lax
from jax.experimental import pallas as pl
from jax.experimental.pallas import tpu as pltpu
from jax.sharding import PartitionSpec as P

BF = jnp.bfloat16
F32 = jnp.float32
VMEM_LIMIT = 8 * 1024 * 1024
LARGE_LIMIT = 58 * 1024 * 1024


def dot(a, b):
    return lax.dot_general(a, b, (((1,), (0,)), ((), ())), preferred_element_type=F32)


def dot_first(a, b):
    return lax.dot_general(a, b, (((0,), (0,)), ((), ())), preferred_element_type=F32)


def dot_last(a, b):
    return lax.dot_general(a, b, (((1,), (1,)), ((), ())), preferred_element_type=F32)


def spread(block, chunks, row):
    for col in range(4):
        chunks[pl.ds(row * 4 + col, 64, stride=16), :] = block[pl.ds(col, 64, stride=4), :]


def collect(chunks, block, row):
    for col in range(4):
        block[pl.ds(col, 64, stride=4), :] = chunks[pl.ds(row * 4 + col, 64, stride=16), :]


def moves(pairs, sems):
    copies = [pltpu.make_async_copy(source, to, sems.at[i]) for i, (source, to) in enumerate(pairs)]
    for copy in copies:
        copy.start()
    return copies


def choose(act, refs, offsets, layer, to, sem):
    index = lax.axis_index("segment")
    for ref, offset in zip(refs, offsets):
        @pl.when((index + offset) % 4 == layer)
        def _():
            getattr(pltpu.make_async_copy(ref, to, sem), act)()


def parts_kernel(inputs, scale, shift, tops, *refs):
    outs, upstream, both, vectors, sems = refs[:4], refs[4], refs[5], refs[6], refs[7]
    index = lax.axis_index("segment")
    lanes = [pl.ds(pl.multiple_of(((index + step) % 4) * 128, 128), 128) for step in range(4)]
    pairs = [(scale, both.at[0:1, :]), (shift, both.at[1:2, :]), (tops.at[:, lanes[0]], upstream)]
    pairs += [(inputs.at[:, lanes[step]], outs[step].at[:1024, :]) for step in range(4)]
    copies = moves(pairs, sems)
    copies[0].wait()
    copies[1].wait()
    vectors[...] = jnp.zeros_like(vectors)
    for step in range(4):
        for place in range(2):
            left = both[place:place + 1, lanes[step]]
            for term in range(3):
                piece = left.astype(BF).astype(F32)
                vectors[place * 3 + term:place * 3 + term + 1, :] = piece
                left = left - piece
        outs[step][1024:, :] = vectors[...].astype(BF)
    for copy in copies[2:]:
        copy.wait()


def first_kernel(firsts, inputs, out, block, chunks, weights, held, sems):
    copies = moves([(firsts, weights), (inputs, held)], sems)
    for copy in copies:
        copy.wait()
    for part in range(4):
        lanes = slice(part * 128, (part + 1) * 128)
        for row in range(4):
            block[...] = dot(weights[row], held[row * 256:(row + 1) * 256, lanes])
            spread(block, chunks, row)
        out[:, part] = chunks[...].astype(BF).reshape(64, 16, 128)


def gated(inputs, vector, place, rows):
    scale, shift = vector[place, 0:1, :], vector[place, 1:2, :]
    return jax.nn.sigmoid(inputs[place, rows, :].astype(F32) * scale + shift), scale


def gate_kernel(seconds, firsts_cols, upstream, own, near, far, last, out, held, vectors, *scratch):
    block, chunks, wide, mixed, weights, fcols, ups, terms, sems = scratch
    index = lax.axis_index("segment")
    pairs = [(seconds, weights), (firsts_cols, fcols), (upstream, ups)]
    for step, part in enumerate((own, near, far, last)):
        layer = (index + 4 - step) % 4
        pairs += [(part.at[:1024, :], held.at[layer]), (part.at[1024:, :], terms.at[layer])]
    for copy in moves(pairs, sems):
        copy.wait()
    for layer in range(4):
        values = terms[layer].astype(F32)
        vectors[layer, 0:1, :] = values[0:1, :] + (values[1:2, :] + values[2:3, :])
        vectors[layer, 1:2, :] = values[3:4, :] + (values[4:5, :] + values[5:6, :])
    for part in range(4):
        wide[...] = fcols[:, part].reshape(1024, 128).astype(F32)
        for col in range(4):
            rows = pl.ds(col, 256, stride=4)
            mixed[rows, :] = dot(weights[col], wide[rows, :].astype(BF))
        out[:, part] = mixed[...].astype(BF).reshape(64, 16, 128)
    for row in range(4):
        rows = slice(row * 256, (row + 1) * 256)
        gate, _ = gated(held, vectors, 3, rows)
        block[...] = ups[rows, :].astype(F32) * gate
        spread(block, chunks, row)
    out[:, 4] = chunks[...].astype(BF).reshape(64, 16, 128)


def column_kernel(layer, received, own, left, right, across, *rest):
    columns, rest = (rest[:3], rest[3:]) if layer == 0 else ((), rest)
    out, (grads, back, weights, got, sems) = rest[0], rest[-5:]
    picked = rest[1:-5]
    index = lax.axis_index("segment")
    factors = (own, left, right, across)
    choose("start", factors, RING, layer, weights, sems.at[5])
    pairs = [(received.at[:, 4] if layer == 3 else received, got)]
    if layer == 3:
        pairs += [(received.at[:, (index + step) % 4], part) for step, part in enumerate(picked)]
    copies = moves(pairs, sems)
    if layer == 0:
        for step, part in enumerate(picked):
            pick("start", (received,) + columns, step, part, sems.at[1 + step])
    copies[0].wait()
    grads[...] = got[...].reshape(1024, 128).astype(F32)
    choose("wait", factors, RING, layer, weights, sems.at[5])
    for col in range(4):
        rows = pl.ds(col, 256, stride=4)
        back[rows, :] = dot_first(weights[col], grads[rows, :].astype(BF))
    out[...] = back[...].astype(BF).reshape(64, 16, 128)
    for copy in copies[1:]:
        copy.wait()
    if layer == 0:
        for step, part in enumerate(picked):
            pick("wait", (received,) + columns, step, part, sems.at[1 + step])


def pick(act, values, step, to, sem):
    index = lax.axis_index("segment")
    for layer, value in enumerate(values):
        if value is not None:
            @pl.when((index + step) % 4 == layer)
            def _():
                getattr(pltpu.make_async_copy(value, to, sem), act)()


def second_kernel(firsts_cols, own, near, far, last, out, grads, firsts_out):
    index = lax.axis_index("segment")
    for step, received in enumerate((own, near, far, last)):
        grads[...] = received[...].reshape(1024, 128).astype(F32)
        firsts_out[...] = firsts_cols[:, (index + 4 - step) % 4].reshape(1024, 128).astype(F32)
        for col in range(4):
            rows = pl.ds(col, 256, stride=4)
            part = dot_last(grads[rows, :].astype(BF), firsts_out[rows, :].astype(BF))
            out[col] = part if step == 0 else out[col] + part


def row_kernel(layer, received, own, left, right, across, upstream, held, vectors, *rest):
    slots, rest = rest[:4], rest[4:]
    earlier, rest = ((None,) + rest[:3], rest[3:]) if layer == 0 else ((), rest)
    outs, rest = (rest[:4], rest[4:]) if layer == 0 else (rest[:2], rest[2:])
    chunks, mixed_chunks, block, mixed_block, next_chunks, vector, weights, inputs, ups, mixed, got, sems = rest
    index = lax.axis_index("segment")
    factors = (own, left, right, across)
    pairs = [(received, got), (upstream, ups), (vectors, vector), (held.at[layer], inputs.at[layer])]
    if layer > 0:
        pairs.append((held.at[layer - 1], inputs.at[layer - 1]))
    copies = moves(pairs, sems)
    choose("start", slots, (0, 3, 2, 1), layer, mixed, sems.at[5])
    choose("start", factors, RING, layer, weights, sems.at[6])
    if layer == 0:
        for step in range(4):
            pick("start", earlier, step, outs[step], sems.at[7 + step])
    copies[0].wait()
    chunks[...] = got[...].reshape(1024, 128).astype(F32)
    choose("wait", slots, (0, 3, 2, 1), layer, mixed, sems.at[5])
    mixed_chunks[...] = mixed[...].reshape(1024, 128).astype(F32)
    choose("wait", factors, RING, layer, weights, sems.at[6])
    for copy in copies[1:]:
        copy.wait()
    for row in range(4):
        rows = slice(row * 256, (row + 1) * 256)
        collect(chunks, block, row)
        collect(mixed_chunks, mixed_block, row)
        through = dot_first(weights[row], block[...].astype(BF))
        up = ups[rows, :].astype(F32)
        gate, scale = gated(inputs, vector, layer, rows)
        slope = (up * gate * (1.0 - gate)).astype(BF).astype(F32)
        gate_grad = (slope * mixed_block[...]).astype(BF).astype(F32)
        result = (up + through + gate_grad * scale).astype(BF)
        if layer == 0:
            for step in range(4):
                @pl.when((index + step) % 4 == 0)
                def _():
                    outs[step][rows, :] = result
        else:
            outs[0][rows, :] = result
            gate, _ = gated(inputs, vector, layer - 1, rows)
            block[...] = result.astype(F32) * gate
            spread(block, next_chunks, row)
    if layer > 0:
        outs[1][...] = next_chunks[...].astype(BF).reshape(64, 16, 128)
    else:
        for step in range(4):
            pick("wait", earlier, step, outs[step], sems.at[7 + step])


def final_kernel(own, near, far, last, out):
    index = lax.axis_index("segment")
    for step, value in enumerate((own, near, far, last)):
        lanes = pl.ds(pl.multiple_of(((index + 4 - step) % 4) * 128, 128), 128)
        out[:, lanes] = value[...]


IN_VMEM = pl.BlockSpec(memory_space=pltpu.VMEM)
ANYWHERE = pl.BlockSpec(memory_space=pl.ANY)


def call(kernel, count, out_shapes, scratch, flops, copies=0, grant=VMEM_LIMIT):
    outs = [jax.ShapeDtypeStruct(s, d) for s, d in out_shapes]
    single = len(outs) == 1
    return pl.pallas_call(
        kernel,
        in_specs=[ANYWHERE if copies else IN_VMEM] * count,
        out_shape=outs[0] if single else outs,
        out_specs=IN_VMEM if single else [IN_VMEM] * len(outs),
        scratch_shapes=[pltpu.VMEM(*s) if isinstance(s[0], tuple) else pltpu.VMEM(s, F32) for s in scratch]
        + ([pltpu.SemaphoreType.DMA((copies,))] if copies else []),
        compiler_params=pltpu.CompilerParams(vmem_limit_bytes=grant),
        cost_estimate=pl.CostEstimate(flops=flops, bytes_accessed=2 << 20, transcendentals=0),
    )


RING = (0, 3, 1, 2)
TALL = (1024, 128)
CHUNKS = (64, 16, 128)
BLOCK = (256, 128)
FLOPS = 2 * 4 * 256 * 256 * 128


FACTOR = ((4, 256, 256), BF)


def passed(value, step):
    return lax.ppermute(value, "segment", [(i, (i + step) % 4) for i in range(4)])


def exchanged(parts):
    return [parts[0]] + [passed(parts[step], step) for step in (1, 2, 3)]


def body(layer_inputs, first_blocks, second_blocks, gate_scale, gate_shift, top_grads):
    firsts, seconds = first_blocks[0], second_blocks[0]
    made = call(
        parts_kernel,
        4,
        [((1040, 128), BF)] * 4 + [(TALL, BF)],
        [(2, 512), (16, 128)],
        1 << 20,
        copies=7,
        grant=LARGE_LIMIT,
    )(layer_inputs[0], gate_scale, gate_shift, top_grads)
    parts, upstream = exchanged(made[:4]), made[4]
    firsts_out = call(
        first_kernel,
        2,
        [((64, 4, 16, 128), BF)],
        [BLOCK, TALL, FACTOR, ((1024, 512), BF)],
        4 * FLOPS,
        copies=2,
        grant=LARGE_LIMIT,
    )(firsts, layer_inputs[0])
    firsts_cols = lax.all_to_all(firsts_out, "seq", 0, 0, tiled=True)
    firsts_cols, parts, firsts, seconds = lax.optimization_barrier((firsts_cols, parts, firsts, seconds))
    payload, held, vectors = call(
        gate_kernel,
        7,
        [((64, 5, 16, 128), BF), ((4, 1024, 128), BF), ((4, 2, 128), F32)],
        [BLOCK, TALL, TALL, TALL, FACTOR, ((64, 4, 16, 128), BF), (TALL, BF), ((4, 16, 128), BF)],
        4 * FLOPS,
        copies=11,
        grant=LARGE_LIMIT,
    )(seconds, firsts_cols, upstream, *parts)
    columns = [None] * 4
    columns[3] = lax.all_to_all(payload, "seq", 0, 0, tiled=True)
    firsts_all = [firsts, passed(firsts, 1), passed(firsts, 3)]
    seconds_all = [seconds, passed(seconds, 1), passed(seconds, 3)]
    firsts_all.append(passed(firsts_all[2], 3))
    seconds_all.append(passed(seconds_all[1], 1))
    columns[3], firsts_all, seconds_all = lax.optimization_barrier((columns[3], firsts_all, seconds_all))

    results, mixed = [None] * 4, None
    for l in (3, 2, 1, 0):
        grant = LARGE_LIMIT if l in (3, 0) else VMEM_LIMIT
        if l < 3:
            columns[l] = lax.all_to_all(sends, "seq", 0, 0, tiled=True)
        operands = [columns[l], *seconds_all] + (columns[1:3] + [grads_three] if l == 0 else [])
        made = call(
            functools.partial(column_kernel, l),
            len(operands),
            [(CHUNKS, BF)] * (5 if l in (3, 0) else 1),
            [TALL, TALL, FACTOR, (CHUNKS, BF)],
            FLOPS,
            copies=6,
            grant=grant,
        )(*operands)
        back = made[0] if l in (3, 0) else made
        received = lax.all_to_all(back, "seq", 0, 0, tiled=True)
        if l == 3:
            mixed = exchanged(made[1:])
            grads_three = columns[3][:, 4]
        if l == 0:
            grads = exchanged(made[1:])
        operands = [received, *firsts_all, upstream, held, vectors, *mixed] + (results[1:] if l == 0 else [])
        made = call(
            functools.partial(row_kernel, l),
            len(operands),
            [(TALL, BF), (CHUNKS, BF)] if l > 0 else [(TALL, BF)] * 4,
            [TALL, TALL, BLOCK, BLOCK, TALL, (4, 2, 128)]
            + [FACTOR, ((4, 1024, 128), BF), (TALL, BF), (CHUNKS, BF), (CHUNKS, BF)],
            FLOPS,
            copies=11,
            grant=grant,
        )(*operands)
        if l > 0:
            upstream, sends = made
            results[l] = upstream

    second = call(second_kernel, 5, [((4, 256, 256), F32)], [TALL, TALL], 4 * FLOPS)(firsts_cols, *grads)
    grads_out = call(final_kernel, 4, [((1024, 512), BF)], [], 1 << 20)(*exchanged(made))
    return grads_out[None], second[None]


def solution(mesh):
    placed = (
        P("segment", "seq", None),
        P("segment", "seq", None, None),
        P("segment", "seq", None, None),
        P("segment", None),
        P("segment", None),
        P("seq", None),
    )
    return jax.shard_map(
        body,
        mesh=mesh,
        in_specs=placed,
        out_specs=(P("segment", "seq", None), P("segment", "seq", None, None)),
        check_vma=False,
    )
```

```python
import functools

import jax
import jax.numpy as jnp
from jax import lax
from jax.experimental import pallas as pl
from jax.experimental.pallas import tpu as pltpu
from jax.sharding import PartitionSpec as P

BF = jnp.bfloat16
F32 = jnp.float32
VMEM_LIMIT = 8 * 1024 * 1024
LARGE_LIMIT = 58 * 1024 * 1024


def dot(a, b):
    return lax.dot_general(a, b, (((1,), (0,)), ((), ())), preferred_element_type=F32)


def dot_first(a, b):
    return lax.dot_general(a, b, (((0,), (0,)), ((), ())), preferred_element_type=F32)


def dot_last(a, b):
    return lax.dot_general(a, b, (((1,), (1,)), ((), ())), preferred_element_type=F32)


def spread(block, chunks, row):
    for col in range(4):
        chunks[pl.ds(row * 4 + col, 64, stride=16), :] = block[pl.ds(col, 64, stride=4), :]


def collect(chunks, block, row):
    for col in range(4):
        block[pl.ds(col, 64, stride=4), :] = chunks[pl.ds(row * 4 + col, 64, stride=16), :]


def moves(pairs, sems):
    copies = [pltpu.make_async_copy(source, to, sems.at[i]) for i, (source, to) in enumerate(pairs)]
    for copy in copies:
        copy.start()
    return copies


def choose(act, refs, offsets, layer, to, sem):
    index = lax.axis_index("segment")
    for ref, offset in zip(refs, offsets):
        @pl.when((index + offset) % 4 == layer)
        def _():
            getattr(pltpu.make_async_copy(ref, to, sem), act)()


def parts_kernel(inputs, scale, shift, tops, *refs):
    outs, upstream, both, vectors, sems = refs[:4], refs[4], refs[5], refs[6], refs[7]
    index = lax.axis_index("segment")
    lanes = [pl.ds(pl.multiple_of(((index + step) % 4) * 128, 128), 128) for step in range(4)]
    pairs = [(scale, both.at[0:1, :]), (shift, both.at[1:2, :]), (tops.at[:, lanes[0]], upstream)]
    pairs += [(inputs.at[:, lanes[step]], outs[step].at[:1024, :]) for step in range(4)]
    copies = moves(pairs, sems)
    copies[0].wait()
    copies[1].wait()
    vectors[...] = jnp.zeros_like(vectors)
    for step in range(4):
        for place in range(2):
            left = both[place:place + 1, lanes[step]]
            for term in range(3):
                piece = left.astype(BF).astype(F32)
                vectors[place * 3 + term:place * 3 + term + 1, :] = piece
                left = left - piece
        outs[step][1024:, :] = vectors[...].astype(BF)
    for copy in copies[2:]:
        copy.wait()


def first_kernel(firsts, inputs, out, block, chunks, weights, held, sems):
    copies = moves(
        [(firsts.at[row], weights.at[row]) for row in range(4)]
        + [(inputs.at[row], held.at[row]) for row in range(4)],
        sems,
    )
    for copy in copies:
        copy.wait()
    for part in range(4):
        lanes = slice(part * 128, (part + 1) * 128)
        for row in range(4):
            block[...] = dot(weights[row], held[row, :, lanes])
            spread(block, chunks, row)
        out[:, part] = chunks[...].astype(BF).reshape(64, 16, 128)


def gated(inputs, place, vectors, layer, rows):
    scale, shift = vectors[layer, 0:1, :], vectors[layer, 1:2, :]
    return jax.nn.sigmoid(inputs[place, rows, :].astype(F32) * scale + shift), scale


def gate_kernel(seconds, firsts_cols, upstream, own, near, far, last, out, held, vectors, *scratch):
    block, chunks, wide, mixed, weights, fcols, ups, terms, sems = scratch
    index = lax.axis_index("segment")
    pairs = [(seconds, weights), (firsts_cols, fcols), (upstream, ups)]
    for step, part in enumerate((own, near, far, last)):
        layer = (index + 4 - step) % 4
        pairs += [(part.at[:1024, :], held.at[layer]), (part.at[1024:, :], terms.at[layer])]
    copies = moves(pairs, sems)
    copies[0].wait()
    copies[1].wait()
    for part in range(4):
        wide[...] = fcols[:, part].reshape(1024, 128).astype(F32)
        for col in range(4):
            rows = pl.ds(col, 256, stride=4)
            mixed[rows, :] = dot(weights[col], wide[rows, :].astype(BF))
        out[:, part] = mixed[...].astype(BF).reshape(64, 16, 128)
    for copy in copies[2:]:
        copy.wait()
    for layer in range(4):
        values = terms[layer].astype(F32)
        vectors[layer, 0:1, :] = values[0:1, :] + (values[1:2, :] + values[2:3, :])
        vectors[layer, 1:2, :] = values[3:4, :] + (values[4:5, :] + values[5:6, :])
    for row in range(4):
        rows = slice(row * 256, (row + 1) * 256)
        gate, _ = gated(held, 3, vectors, 3, rows)
        block[...] = ups[rows, :].astype(F32) * gate
        spread(block, chunks, row)
    out[:, 4] = chunks[...].astype(BF).reshape(64, 16, 128)


def column_kernel(layer, received, own, left, right, across, *rest):
    columns, rest = (rest[:3], rest[3:]) if layer == 0 else ((), rest)
    if layer == 0:
        columns = columns[:2] + (columns[2].at[:, 4],)
    out, (grads, back, weights, got, sems) = rest[0], rest[-5:]
    picked = rest[1:-5]
    index = lax.axis_index("segment")
    factors = (own, left, right, across)
    choose("start", factors, RING, layer, weights, sems.at[5])
    pairs = [(received.at[:, 4] if layer == 3 else received, got)]
    if layer == 3:
        pairs += [(received.at[:, (index + step) % 4], part) for step, part in enumerate(picked)]
    copies = moves(pairs, sems)
    if layer == 0:
        for step, part in enumerate(picked):
            pick("start", (received,) + columns, step, part, sems.at[1 + step])
    copies[0].wait()
    grads[...] = got[...].reshape(1024, 128).astype(F32)
    choose("wait", factors, RING, layer, weights, sems.at[5])
    for col in range(4):
        rows = pl.ds(col, 256, stride=4)
        back[rows, :] = dot_first(weights[col], grads[rows, :].astype(BF))
    out[...] = back[...].astype(BF).reshape(64, 16, 128)
    for copy in copies[1:]:
        copy.wait()
    if layer == 0:
        for step, part in enumerate(picked):
            pick("wait", (received,) + columns, step, part, sems.at[1 + step])


def pick(act, values, step, to, sem):
    index = lax.axis_index("segment")
    for layer, value in enumerate(values):
        if value is not None:
            @pl.when((index + step) % 4 == layer)
            def _():
                getattr(pltpu.make_async_copy(value, to, sem), act)()


def second_kernel(firsts_cols, own, near, far, last, out, grads, firsts_out):
    index = lax.axis_index("segment")
    for step, received in enumerate((own, near, far, last)):
        grads[...] = received[...].reshape(1024, 128).astype(F32)
        firsts_out[...] = firsts_cols[:, (index + 4 - step) % 4].reshape(1024, 128).astype(F32)
        for col in range(4):
            rows = pl.ds(col, 256, stride=4)
            part = dot_last(grads[rows, :].astype(BF), firsts_out[rows, :].astype(BF))
            out[col] = part if step == 0 else out[col] + part


def row_kernel(layer, received, upstream, held, vectors, own, left, right, across, *rest):
    slots, rest = (rest[:4], rest[4:]) if layer == 3 else (rest[0], rest[1:])
    earlier, rest = ((None,) + rest[:3], rest[3:]) if layer == 0 else ((), rest)
    outs, rest = (rest[:4], rest[4:]) if layer == 0 else (rest[:2], rest[2:])
    kept, rest = (rest[:3], rest[3:]) if layer == 3 else ((), rest)
    chunks, mixed_chunks, block, mixed_block, next_chunks, weights = rest[:6]
    sems = rest[-1]
    index = lax.axis_index("segment")
    factors = (own, left, right, across)
    choose("start", factors, RING, layer, weights, sems.at[0])
    place = layer
    if layer in (3, 0):
        got, ups = rest[6:8]
        pairs = [(received, got), (upstream, ups)]
        if layer == 3:
            mixed, inputs, vector = kept
            for step, part in enumerate(slots):
                pairs.append((part, mixed.at[(index + 4 - step) % 4]))
            pairs += [(held, inputs), (vectors, vector)]
        else:
            place = 0
            mixed, inputs, vector = rest[8:11]
            pairs += [(slots.at[0:1], mixed), (held.at[0:1], inputs), (vectors, vector)]
        copies = moves(pairs, sems.at[5:])
        for step in range(len(earlier)):
            pick("start", earlier, step, outs[step], sems.at[1 + step])
        copies[0].wait()
        received, upstream, held, vectors = got, ups, inputs, vector
    else:
        mixed = slots
    chunks[...] = received[...].reshape(1024, 128).astype(F32)
    if layer in (3, 0):
        for copy in copies[1:]:
            copy.wait()
    mixed_chunks[...] = mixed[place].reshape(1024, 128).astype(F32)
    choose("wait", factors, RING, layer, weights, sems.at[0])
    for row in range(4):
        rows = slice(row * 256, (row + 1) * 256)
        collect(chunks, block, row)
        collect(mixed_chunks, mixed_block, row)
        through = dot_first(weights[row], block[...].astype(BF))
        up = upstream[rows, :].astype(F32)
        gate, scale = gated(held, place, vectors, layer, rows)
        slope = (up * gate * (1.0 - gate)).astype(BF).astype(F32)
        gate_grad = (slope * mixed_block[...]).astype(BF).astype(F32)
        result = (up + through + gate_grad * scale).astype(BF)
        if layer == 0:
            for step in range(4):
                @pl.when((index + step) % 4 == 0)
                def _():
                    outs[step][rows, :] = result
        else:
            outs[0][rows, :] = result
            gate, _ = gated(held, place - 1, vectors, layer - 1, rows)
            block[...] = result.astype(F32) * gate
            spread(block, next_chunks, row)
    if layer > 0:
        outs[1][...] = next_chunks[...].astype(BF).reshape(64, 16, 128)
    else:
        for step in range(4):
            pick("wait", earlier, step, outs[step], sems.at[1 + step])


def middle_kernel(layer, received, upstream, held, vectors, mixed, own, left, right, across, *rest):
    row_kernel(layer, received, upstream, held, vectors, own, left, right, across, mixed, *rest)


def final_kernel(own, near, far, last, out):
    index = lax.axis_index("segment")
    for step, value in enumerate((own, near, far, last)):
        lanes = pl.ds(pl.multiple_of(((index + 4 - step) % 4) * 128, 128), 128)
        out[:, lanes] = value[...]


IN_VMEM = pl.BlockSpec(memory_space=pltpu.VMEM)
ANYWHERE = pl.BlockSpec(memory_space=pl.ANY)


def call(kernel, count, out_shapes, scratch, flops, anywhere=0, copies=0, grant=VMEM_LIMIT):
    outs = [jax.ShapeDtypeStruct(s, d) for s, d in out_shapes]
    single = len(outs) == 1
    return pl.pallas_call(
        kernel,
        in_specs=[IN_VMEM] * (count - anywhere) + [ANYWHERE] * anywhere,
        out_shape=outs[0] if single else outs,
        out_specs=IN_VMEM if single else [IN_VMEM] * len(outs),
        scratch_shapes=[pltpu.VMEM(*s) if isinstance(s[0], tuple) else pltpu.VMEM(s, F32) for s in scratch]
        + ([pltpu.SemaphoreType.DMA((copies,))] if copies else []),
        compiler_params=pltpu.CompilerParams(vmem_limit_bytes=grant),
        cost_estimate=pl.CostEstimate(flops=flops, bytes_accessed=2 << 20, transcendentals=0),
    )


RING = (0, 3, 1, 2)
TALL = (1024, 128)
CHUNKS = (64, 16, 128)
BLOCK = (256, 128)
FLOPS = 2 * 4 * 256 * 256 * 128


FACTOR = ((4, 256, 256), BF)


def passed(value, step):
    return lax.ppermute(value, "segment", [(i, (i + step) % 4) for i in range(4)])


def exchanged(parts):
    return [parts[0]] + [passed(parts[step], step) for step in (1, 2, 3)]


def body(layer_inputs, first_blocks, second_blocks, gate_scale, gate_shift, top_grads):
    firsts, seconds = first_blocks[0], second_blocks[0]
    made = call(
        parts_kernel,
        4,
        [((1040, 128), BF)] * 4 + [(TALL, BF)],
        [(2, 512), (16, 128)],
        1 << 20,
        anywhere=4,
        copies=7,
        grant=LARGE_LIMIT,
    )(layer_inputs[0], gate_scale, gate_shift, top_grads)
    parts, upstream = exchanged(made[:4]), made[4]
    firsts_out = call(
        first_kernel,
        2,
        [((64, 4, 16, 128), BF)],
        [BLOCK, TALL, FACTOR, ((4, 256, 512), BF)],
        4 * FLOPS,
        anywhere=2,
        copies=8,
        grant=LARGE_LIMIT,
    )(firsts, layer_inputs[0].reshape(4, 256, 512))
    firsts_cols = lax.all_to_all(firsts_out, "seq", 0, 0, tiled=True)
    seconds_all = [seconds, passed(seconds, 1), passed(seconds, 3)]
    firsts_cols, parts, firsts, seconds_all = lax.optimization_barrier(
        (firsts_cols, parts, firsts, seconds_all)
    )
    payload, held, vectors = call(
        gate_kernel,
        7,
        [((64, 5, 16, 128), BF), ((4, 1024, 128), BF), ((4, 2, 128), F32)],
        [BLOCK, TALL, TALL, TALL, FACTOR, ((64, 4, 16, 128), BF), (TALL, BF), ((4, 16, 128), BF)],
        4 * FLOPS,
        anywhere=7,
        copies=11,
        grant=LARGE_LIMIT,
    )(seconds_all[0], firsts_cols, upstream, *parts)
    columns = [None] * 4
    columns[3] = lax.all_to_all(payload, "seq", 0, 0, tiled=True)
    firsts_all = [firsts, passed(firsts, 1), passed(firsts, 3)]
    firsts_all.append(passed(firsts_all[2], 3))
    seconds_all.append(passed(seconds_all[1], 1))
    columns[3], firsts_all, seconds_all = lax.optimization_barrier((columns[3], firsts_all, seconds_all))

    results, mixed = [None] * 4, None
    for l in (3, 2, 1, 0):
        grant = LARGE_LIMIT if l in (3, 0) else VMEM_LIMIT
        if l < 3:
            columns[l] = lax.all_to_all(sends, "seq", 0, 0, tiled=True)
        operands = [columns[l], *seconds_all] + (columns[1:] if l == 0 else [])
        made = call(
            functools.partial(column_kernel, l),
            len(operands),
            [(CHUNKS, BF)] * (5 if l in (3, 0) else 1),
            [TALL, TALL, FACTOR, (CHUNKS, BF)],
            FLOPS,
            anywhere=len(operands),
            copies=6,
            grant=LARGE_LIMIT if l == 3 else VMEM_LIMIT,
        )(*operands)
        back = made[0] if l in (3, 0) else made
        received = lax.all_to_all(back, "seq", 0, 0, tiled=True)
        if l == 3:
            mixed = exchanged(made[1:])
        if l == 0:
            grads = exchanged(made[1:])
        operands = [received, upstream, held, vectors, *firsts_all]
        operands += (mixed if l == 3 else [mixed]) + (results[1:] if l == 0 else [])
        outs = [(TALL, BF), (CHUNKS, BF)] if l > 0 else [(TALL, BF)] * 4
        scratch = [TALL, TALL, BLOCK, BLOCK, TALL, FACTOR]
        if l in (3, 0):
            scratch += [(CHUNKS, BF), (TALL, BF)]
        if l == 3:
            outs += [((4,) + CHUNKS, BF), ((4, 1024, 128), BF), ((4, 2, 128), F32)]
        if l == 0:
            scratch += [((1,) + CHUNKS, BF), ((1, 1024, 128), BF), (4, 2, 128)]
        order = [0, 1, 2, 3] + [8] * (l in (2, 1)) + [4, 5, 6, 7] + list(range(8 + (l in (2, 1)), len(operands)))
        made = call(
            functools.partial(row_kernel, l) if l in (3, 0) else functools.partial(middle_kernel, l),
            len(operands),
            outs,
            scratch,
            FLOPS,
            anywhere=len(operands) if l in (3, 0) else 4,
            copies=14,
            grant=grant,
        )(*[operands[i] for i in order])
        if l == 3:
            mixed, held, vectors = made[2:]
            made = made[:2]
        if l > 0:
            upstream, sends = made
            results[l] = upstream

    second = call(second_kernel, 5, [((4, 256, 256), F32)], [TALL, TALL], 4 * FLOPS)(firsts_cols, *grads)
    grads_out = call(final_kernel, 4, [((1024, 512), BF)], [], 1 << 20)(*exchanged(made))
    return grads_out[None], second[None]


def solution(mesh):
    placed = (
        P("segment", "seq", None),
        P("segment", "seq", None, None),
        P("segment", "seq", None, None),
        P("segment", None),
        P("segment", None),
        P("seq", None),
    )
    return jax.shard_map(
        body,
        mesh=mesh,
        in_specs=placed,
        out_specs=(P("segment", "seq", None), P("segment", "seq", None, None)),
        check_vma=False,
    )
```

```python
import functools

import jax
import jax.numpy as jnp
from jax import lax
from jax.experimental import pallas as pl
from jax.experimental.pallas import tpu as pltpu
from jax.sharding import PartitionSpec as P

BF = jnp.bfloat16
F32 = jnp.float32
VMEM_LIMIT = 8 * 1024 * 1024
LARGE_LIMIT = 58 * 1024 * 1024


def dot(a, b):
    return lax.dot_general(a, b, (((1,), (0,)), ((), ())), preferred_element_type=F32)


def dot_first(a, b):
    return lax.dot_general(a, b, (((0,), (0,)), ((), ())), preferred_element_type=F32)


def dot_last(a, b):
    return lax.dot_general(a, b, (((1,), (1,)), ((), ())), preferred_element_type=F32)


def spread(block, chunks, row):
    for col in range(4):
        chunks[pl.ds(row * 4 + col, 64, stride=16), :] = block[pl.ds(col, 64, stride=4), :]


def collect(chunks, block, row):
    for col in range(4):
        block[pl.ds(col, 64, stride=4), :] = chunks[pl.ds(row * 4 + col, 64, stride=16), :]


def moves(pairs, sems):
    copies = [pltpu.make_async_copy(source, to, sems.at[i]) for i, (source, to) in enumerate(pairs)]
    for copy in copies:
        copy.start()
    return copies


def choose(act, refs, offsets, layer, to, sem):
    index = lax.axis_index("segment")
    for ref, offset in zip(refs, offsets):
        @pl.when((index + offset) % 4 == layer)
        def _():
            getattr(pltpu.make_async_copy(ref, to, sem), act)()


def parts_kernel(inputs, scale, shift, tops, *refs):
    outs, upstream, both, vectors, sems = refs[:4], refs[4], refs[5], refs[6], refs[7]
    index = lax.axis_index("segment")
    lanes = [pl.ds(pl.multiple_of(((index + step) % 4) * 128, 128), 128) for step in range(4)]
    pairs = [(scale, both.at[0:1, :]), (shift, both.at[1:2, :]), (tops.at[:, lanes[0]], upstream)]
    pairs += [(inputs.at[:, lanes[step]], outs[step].at[:1024, :]) for step in range(4)]
    copies = moves(pairs, sems)
    copies[0].wait()
    copies[1].wait()
    vectors[...] = jnp.zeros_like(vectors)
    for step in range(4):
        for place in range(2):
            left = both[place:place + 1, lanes[step]]
            for term in range(3):
                piece = left.astype(BF).astype(F32)
                vectors[place * 3 + term:place * 3 + term + 1, :] = piece
                left = left - piece
        outs[step][1024:, :] = vectors[...].astype(BF)
    for copy in copies[2:]:
        copy.wait()


def first_kernel(firsts, inputs, out, block, chunks, weights, held, done, sems):
    copies = moves([(firsts, weights), (inputs, held)], sems)
    for copy in copies:
        copy.wait()
    written = []
    for part in range(4):
        lanes = slice(part * 128, (part + 1) * 128)
        for row in range(4):
            block[...] = dot(weights[row], held[row, :, lanes])
            spread(block, chunks, row)
        done[part] = chunks[...].astype(BF).reshape(64, 16, 128)
        written.append(pltpu.make_async_copy(done.at[part], out.at[:, part], sems.at[2 + part]))
        written[-1].start()
    for copy in written:
        copy.wait()


def gated(inputs, place, vectors, layer, rows):
    scale, shift = vectors[layer, 0:1, :], vectors[layer, 1:2, :]
    return jax.nn.sigmoid(inputs[place, rows, :].astype(F32) * scale + shift), scale


def gate_kernel(seconds, firsts_cols, upstream, own, near, far, last, out, held, vectors, *scratch):
    block, chunks, wide, mixed, weights, fcols, ups, terms, sems = scratch
    index = lax.axis_index("segment")
    pairs = [(seconds, weights), (firsts_cols, fcols), (upstream, ups)]
    for step, part in enumerate((own, near, far, last)):
        layer = (index + 4 - step) % 4
        pairs += [(part.at[:1024, :], held.at[layer]), (part.at[1024:, :], terms.at[layer])]
    copies = moves(pairs, sems)
    copies[0].wait()
    copies[1].wait()
    for part in range(4):
        wide[...] = fcols[:, part].reshape(1024, 128).astype(F32)
        for col in range(4):
            rows = pl.ds(col, 256, stride=4)
            mixed[rows, :] = dot(weights[col], wide[rows, :].astype(BF))
        out[:, part] = mixed[...].astype(BF).reshape(64, 16, 128)
    for copy in copies[2:]:
        copy.wait()
    for layer in range(4):
        values = terms[layer].astype(F32)
        vectors[layer, 0:1, :] = values[0:1, :] + (values[1:2, :] + values[2:3, :])
        vectors[layer, 1:2, :] = values[3:4, :] + (values[4:5, :] + values[5:6, :])
    for row in range(4):
        rows = slice(row * 256, (row + 1) * 256)
        gate, _ = gated(held, 3, vectors, 3, rows)
        block[...] = ups[rows, :].astype(F32) * gate
        spread(block, chunks, row)
    out[:, 4] = chunks[...].astype(BF).reshape(64, 16, 128)


def column_kernel(layer, received, own, left, right, across, *rest):
    columns, rest = (rest[:3], rest[3:]) if layer == 0 else ((), rest)
    if layer == 0:
        columns = columns[:2] + (columns[2].at[:, 4],)
    out, (grads, back, weights, got, sems) = rest[0], rest[-5:]
    picked = rest[1:-5]
    index = lax.axis_index("segment")
    factors = (own, left, right, across)
    choose("start", factors, RING, layer, weights, sems.at[5])
    pairs = [(received.at[:, 4] if layer == 3 else received, got)]
    if layer == 3:
        pairs += [(received.at[:, (index + step) % 4], part) for step, part in enumerate(picked)]
    copies = moves(pairs, sems)
    if layer == 0:
        for step, part in enumerate(picked):
            pick("start", (received,) + columns, step, part, sems.at[1 + step])
    copies[0].wait()
    grads[...] = got[...].reshape(1024, 128).astype(F32)
    choose("wait", factors, RING, layer, weights, sems.at[5])
    for col in range(4):
        rows = pl.ds(col, 256, stride=4)
        back[rows, :] = dot_first(weights[col], grads[rows, :].astype(BF))
    out[...] = back[...].astype(BF).reshape(64, 16, 128)
    for copy in copies[1:]:
        copy.wait()
    if layer == 0:
        for step, part in enumerate(picked):
            pick("wait", (received,) + columns, step, part, sems.at[1 + step])


def pick(act, values, step, to, sem):
    index = lax.axis_index("segment")
    for layer, value in enumerate(values):
        if value is not None:
            @pl.when((index + step) % 4 == layer)
            def _():
                getattr(pltpu.make_async_copy(value, to, sem), act)()


def second_kernel(firsts_cols, own, near, far, last, out, grads, firsts_out):
    index = lax.axis_index("segment")
    for step, received in enumerate((own, near, far, last)):
        grads[...] = received[...].reshape(1024, 128).astype(F32)
        firsts_out[...] = firsts_cols[:, (index + 4 - step) % 4].reshape(1024, 128).astype(F32)
        for col in range(4):
            rows = pl.ds(col, 256, stride=4)
            part = dot_last(grads[rows, :].astype(BF), firsts_out[rows, :].astype(BF))
            out[col] = part if step == 0 else out[col] + part


def row_kernel(layer, received, upstream, held, vectors, own, left, right, across, *rest):
    slots, rest = (rest[:4], rest[4:]) if layer == 3 else (rest[0], rest[1:])
    earlier, rest = ((None,) + rest[:3], rest[3:]) if layer == 0 else ((), rest)
    outs, rest = (rest[:4], rest[4:]) if layer == 0 else (rest[:2], rest[2:])
    kept, rest = (rest[:3], rest[3:]) if layer == 3 else ((), rest)
    chunks, mixed_chunks, block, mixed_block, next_chunks, weights = rest[:6]
    sems = rest[-1]
    index = lax.axis_index("segment")
    factors = (own, left, right, across)
    choose("start", factors, RING, layer, weights, sems.at[0])
    place = layer
    if layer in (3, 0):
        got, ups = rest[6:8]
        pairs = [(received, got), (upstream, ups)]
        if layer == 3:
            mixed, inputs, vector = kept
            for step, part in enumerate(slots):
                pairs.append((part, mixed.at[(index + 4 - step) % 4]))
            pairs += [(held, inputs), (vectors, vector)]
        else:
            place = 0
            mixed, inputs, vector = rest[8:11]
            pairs += [(slots.at[0:1], mixed), (held.at[0:1], inputs), (vectors, vector)]
        copies = moves(pairs, sems.at[5:])
        for step in range(len(earlier)):
            pick("start", earlier, step, outs[step], sems.at[1 + step])
        copies[0].wait()
        received, upstream, held, vectors = got, ups, inputs, vector
    else:
        mixed = slots
    chunks[...] = received[...].reshape(1024, 128).astype(F32)
    if layer in (3, 0):
        for copy in copies[1:]:
            copy.wait()
    mixed_chunks[...] = mixed[place].reshape(1024, 128).astype(F32)
    choose("wait", factors, RING, layer, weights, sems.at[0])
    for row in range(4):
        rows = slice(row * 256, (row + 1) * 256)
        collect(chunks, block, row)
        collect(mixed_chunks, mixed_block, row)
        through = dot_first(weights[row], block[...].astype(BF))
        up = upstream[rows, :].astype(F32)
        gate, scale = gated(held, place, vectors, layer, rows)
        slope = (up * gate * (1.0 - gate)).astype(BF).astype(F32)
        gate_grad = (slope * mixed_block[...]).astype(BF).astype(F32)
        result = (up + through + gate_grad * scale).astype(BF)
        if layer == 0:
            for step in range(4):
                @pl.when((index + step) % 4 == 0)
                def _():
                    outs[step][rows, :] = result
        else:
            outs[0][rows, :] = result
            gate, _ = gated(held, place - 1, vectors, layer - 1, rows)
            block[...] = result.astype(F32) * gate
            spread(block, next_chunks, row)
    if layer > 0:
        outs[1][...] = next_chunks[...].astype(BF).reshape(64, 16, 128)
    else:
        for step in range(4):
            pick("wait", earlier, step, outs[step], sems.at[1 + step])


def middle_kernel(layer, received, upstream, held, vectors, mixed, own, left, right, across, *rest):
    row_kernel(layer, received, upstream, held, vectors, own, left, right, across, mixed, *rest)


def final_kernel(own, near, far, last, out):
    index = lax.axis_index("segment")
    for step, value in enumerate((own, near, far, last)):
        lanes = pl.ds(pl.multiple_of(((index + 4 - step) % 4) * 128, 128), 128)
        out[:, lanes] = value[...]


IN_VMEM = pl.BlockSpec(memory_space=pltpu.VMEM)
ANYWHERE = pl.BlockSpec(memory_space=pl.ANY)


def call(kernel, count, out_shapes, scratch, flops, anywhere=0, copies=0, grant=VMEM_LIMIT, free=()):
    outs = [jax.ShapeDtypeStruct(s, d) for s, d in out_shapes]
    single = len(outs) == 1
    specs = [ANYWHERE if i in free else IN_VMEM for i in range(len(outs))]
    return pl.pallas_call(
        kernel,
        in_specs=[IN_VMEM] * (count - anywhere) + [ANYWHERE] * anywhere,
        out_shape=outs[0] if single else outs,
        out_specs=specs[0] if single else specs,
        scratch_shapes=[pltpu.VMEM(*s) if isinstance(s[0], tuple) else pltpu.VMEM(s, F32) for s in scratch]
        + ([pltpu.SemaphoreType.DMA((copies,))] if copies else []),
        compiler_params=pltpu.CompilerParams(vmem_limit_bytes=grant),
        cost_estimate=pl.CostEstimate(flops=flops, bytes_accessed=2 << 20, transcendentals=0),
    )


RING = (0, 3, 1, 2)
TALL = (1024, 128)
CHUNKS = (64, 16, 128)
BLOCK = (256, 128)
FLOPS = 2 * 4 * 256 * 256 * 128


FACTOR = ((4, 256, 256), BF)


def passed(value, step):
    return lax.ppermute(value, "segment", [(i, (i + step) % 4) for i in range(4)])


def exchanged(parts):
    return [parts[0]] + [passed(parts[step], step) for step in (1, 2, 3)]


def body(layer_inputs, first_blocks, second_blocks, gate_scale, gate_shift, top_grads):
    firsts, seconds = first_blocks[0], second_blocks[0]
    made = call(
        parts_kernel,
        4,
        [((1040, 128), BF)] * 4 + [(TALL, BF)],
        [(2, 512), (16, 128)],
        1 << 20,
        anywhere=4,
        copies=7,
        grant=LARGE_LIMIT,
    )(layer_inputs[0], gate_scale, gate_shift, top_grads)
    parts, upstream = exchanged(made[:4]), made[4]
    firsts_out = call(
        first_kernel,
        2,
        [((64, 4, 16, 128), BF)],
        [BLOCK, TALL, FACTOR, ((4, 256, 512), BF), ((4, 64, 16, 128), BF)],
        4 * FLOPS,
        anywhere=2,
        copies=6,
        free=(0,),
        grant=LARGE_LIMIT,
    )(firsts, layer_inputs[0].reshape(4, 256, 512))
    firsts_cols = lax.all_to_all(firsts_out, "seq", 0, 0, tiled=True)
    right = passed(seconds, 3)
    firsts_cols, parts, firsts, seconds, right = lax.optimization_barrier(
        (firsts_cols, parts, firsts, seconds, right)
    )
    payload, held, vectors = call(
        gate_kernel,
        7,
        [((64, 5, 16, 128), BF), ((4, 1024, 128), BF), ((4, 2, 128), F32)],
        [BLOCK, TALL, TALL, TALL, FACTOR, ((64, 4, 16, 128), BF), (TALL, BF), ((4, 16, 128), BF)],
        4 * FLOPS,
        anywhere=7,
        copies=11,
        grant=LARGE_LIMIT,
    )(seconds, firsts_cols, upstream, *parts)
    columns = [None] * 4
    columns[3] = lax.all_to_all(payload, "seq", 0, 0, tiled=True)
    seconds_all = [seconds, passed(seconds, 1), right, passed(right, 3)]
    firsts_all = [firsts, passed(firsts, 1), passed(firsts, 3)]
    columns[3], firsts_all, seconds_all = lax.optimization_barrier((columns[3], firsts_all, seconds_all))

    results, mixed = [None] * 4, None
    for l in (3, 2, 1, 0):
        grant = LARGE_LIMIT if l in (3, 0) else VMEM_LIMIT
        if l < 3:
            columns[l] = lax.all_to_all(sends, "seq", 0, 0, tiled=True)
        operands = [columns[l], *seconds_all] + (columns[1:] if l == 0 else [])
        made = call(
            functools.partial(column_kernel, l),
            len(operands),
            [(CHUNKS, BF)] * (5 if l in (3, 0) else 1),
            [TALL, TALL, FACTOR, (CHUNKS, BF)],
            FLOPS,
            anywhere=len(operands),
            copies=6,
            grant=LARGE_LIMIT if l == 3 else VMEM_LIMIT,
        )(*operands)
        back = made[0] if l in (3, 0) else made
        received = lax.all_to_all(back, "seq", 0, 0, tiled=True)
        if l == 3:
            mixed = exchanged(made[1:])
            firsts_all.append(passed(firsts_all[2], 3))
        if l == 0:
            grads = exchanged(made[1:])
        operands = [received, upstream, held, vectors, *firsts_all]
        operands += (mixed if l == 3 else [mixed]) + (results[1:] if l == 0 else [])
        outs = [(TALL, BF), (CHUNKS, BF)] if l > 0 else [(TALL, BF)] * 4
        scratch = [TALL, TALL, BLOCK, BLOCK, TALL, FACTOR]
        if l in (3, 0):
            scratch += [(CHUNKS, BF), (TALL, BF)]
        if l == 3:
            outs += [((4,) + CHUNKS, BF), ((4, 1024, 128), BF), ((4, 2, 128), F32)]
        if l == 0:
            scratch += [((1,) + CHUNKS, BF), ((1, 1024, 128), BF), (4, 2, 128)]
        order = [0, 1, 2, 3] + [8] * (l in (2, 1)) + [4, 5, 6, 7] + list(range(8 + (l in (2, 1)), len(operands)))
        made = call(
            functools.partial(row_kernel, l) if l in (3, 0) else functools.partial(middle_kernel, l),
            len(operands),
            outs,
            scratch,
            FLOPS,
            anywhere=len(operands) if l in (3, 0) else 4,
            copies=14,
            grant=grant,
        )(*[operands[i] for i in order])
        if l == 3:
            mixed, held, vectors = made[2:]
            made = made[:2]
        if l > 0:
            upstream, sends = made
            results[l] = upstream

    second = call(second_kernel, 5, [((4, 256, 256), F32)], [TALL, TALL], 4 * FLOPS)(firsts_cols, *grads)
    grads_out = call(final_kernel, 4, [((1024, 512), BF)], [], 1 << 20)(*exchanged(made))
    return grads_out[None], second[None]


def solution(mesh):
    placed = (
        P("segment", "seq", None),
        P("segment", "seq", None, None),
        P("segment", "seq", None, None),
        P("segment", None),
        P("segment", None),
        P("seq", None),
    )
    return jax.shard_map(
        body,
        mesh=mesh,
        in_specs=placed,
        out_specs=(P("segment", "seq", None), P("segment", "seq", None, None)),
        check_vma=False,
    )
```

```python
import functools

import jax
import jax.numpy as jnp
from jax import lax
from jax.experimental import pallas as pl
from jax.experimental.pallas import tpu as pltpu
from jax.sharding import PartitionSpec as P

BF = jnp.bfloat16
F32 = jnp.float32
VMEM_LIMIT = 8 * 1024 * 1024
LARGE_LIMIT = 58 * 1024 * 1024


def dot(a, b):
    return lax.dot_general(a, b, (((1,), (0,)), ((), ())), preferred_element_type=F32)


def dot_first(a, b):
    return lax.dot_general(a, b, (((0,), (0,)), ((), ())), preferred_element_type=F32)


def dot_last(a, b):
    return lax.dot_general(a, b, (((1,), (1,)), ((), ())), preferred_element_type=F32)


def spread(block, chunks, row):
    for col in range(4):
        chunks[pl.ds(row * 4 + col, 64, stride=16), :] = block[pl.ds(col, 64, stride=4), :]


def collect(chunks, block, row):
    for col in range(4):
        block[pl.ds(col, 64, stride=4), :] = chunks[pl.ds(row * 4 + col, 64, stride=16), :]


def moves(pairs, sems):
    copies = [pltpu.make_async_copy(source, to, sems.at[i]) for i, (source, to) in enumerate(pairs)]
    for copy in copies:
        copy.start()
    return copies


def choose(act, refs, offsets, layer, to, sem):
    index = lax.axis_index("segment")
    for ref, offset in zip(refs, offsets):
        @pl.when((index + offset) % 4 == layer)
        def _():
            getattr(pltpu.make_async_copy(ref, to, sem), act)()


def parts_kernel(inputs, scale, shift, tops, *refs):
    outs, upstream, both, vectors, sems = refs[:4], refs[4], refs[5], refs[6], refs[7]
    index = lax.axis_index("segment")
    lanes = [pl.ds(pl.multiple_of(((index + step) % 4) * 128, 128), 128) for step in range(4)]
    pairs = [(scale, both.at[0:1, :]), (shift, both.at[1:2, :]), (tops.at[:, lanes[0]], upstream)]
    pairs += [(inputs.at[:, lanes[step]], outs[step].at[:1024, :]) for step in range(4)]
    copies = moves(pairs, sems)
    copies[0].wait()
    copies[1].wait()
    vectors[...] = jnp.zeros_like(vectors)
    for step in range(4):
        for place in range(2):
            left = both[place:place + 1, lanes[step]]
            for term in range(3):
                piece = left.astype(BF).astype(F32)
                vectors[place * 3 + term:place * 3 + term + 1, :] = piece
                left = left - piece
        outs[step][1024:, :] = vectors[...].astype(BF)
    for copy in copies[2:]:
        copy.wait()


def first_kernel(firsts, inputs, out, block, chunks, weights, held, done, sems):
    copies = moves([(firsts, weights), (inputs, held)], sems)
    for copy in copies:
        copy.wait()
    written = []
    for part in range(4):
        lanes = slice(part * 128, (part + 1) * 128)
        for row in range(4):
            block[...] = dot(weights[row], held[row, :, lanes])
            spread(block, chunks, row)
        done[part] = chunks[...].astype(BF).reshape(64, 16, 128)
        written.append(pltpu.make_async_copy(done.at[part], out.at[:, part], sems.at[2 + part]))
        written[-1].start()
    for copy in written:
        copy.wait()


def gated(inputs, place, vectors, layer, rows):
    scale, shift = vectors[layer, 0:1, :], vectors[layer, 1:2, :]
    return jax.nn.sigmoid(inputs[place, rows, :].astype(F32) * scale + shift), scale


def gate_kernel(seconds, firsts_cols, upstream, own, near, far, last, out, held, vectors, *scratch):
    block, chunks, wide, mixed, weights, fcols, ups, terms, sems = scratch
    index = lax.axis_index("segment")
    pairs = [(seconds, weights), (firsts_cols, fcols), (upstream, ups)]
    for step, part in enumerate((own, near, far, last)):
        layer = (index + 4 - step) % 4
        pairs += [(part.at[:1024, :], held.at[layer]), (part.at[1024:, :], terms.at[layer])]
    copies = moves(pairs, sems)
    copies[0].wait()
    copies[1].wait()
    for part in range(4):
        wide[...] = fcols[:, part].reshape(1024, 128).astype(F32)
        for col in range(4):
            rows = pl.ds(col, 256, stride=4)
            mixed[rows, :] = dot(weights[col], wide[rows, :].astype(BF))
        out[:, part] = mixed[...].astype(BF).reshape(64, 16, 128)
    for copy in copies[2:]:
        copy.wait()
    for layer in range(4):
        values = terms[layer].astype(F32)
        vectors[layer, 0:1, :] = values[0:1, :] + (values[1:2, :] + values[2:3, :])
        vectors[layer, 1:2, :] = values[3:4, :] + (values[4:5, :] + values[5:6, :])
    for row in range(4):
        rows = slice(row * 256, (row + 1) * 256)
        gate, _ = gated(held, 3, vectors, 3, rows)
        block[...] = ups[rows, :].astype(F32) * gate
        spread(block, chunks, row)
    out[:, 4] = chunks[...].astype(BF).reshape(64, 16, 128)


def column_kernel(layer, received, own, left, right, across, *rest):
    columns, rest = (rest[:3], rest[3:]) if layer == 0 else ((), rest)
    if layer == 0:
        columns = columns[:2] + (columns[2].at[:, 4],)
    out, (grads, back, weights, got, sems) = rest[0], rest[-5:]
    picked = rest[1:-5]
    index = lax.axis_index("segment")
    factors = (own, left, right, across)
    choose("start", factors, RING, layer, weights, sems.at[5])
    pairs = [(received.at[:, 4] if layer == 3 else received, got)]
    if layer == 3:
        pairs += [(received.at[:, (index + step) % 4], part) for step, part in enumerate(picked)]
    copies = moves(pairs, sems)
    if layer == 0:
        for step, part in enumerate(picked):
            pick("start", (received,) + columns, step, part, sems.at[1 + step])
    copies[0].wait()
    grads[...] = got[...].reshape(1024, 128).astype(F32)
    choose("wait", factors, RING, layer, weights, sems.at[5])
    for col in range(4):
        rows = pl.ds(col, 256, stride=4)
        back[rows, :] = dot_first(weights[col], grads[rows, :].astype(BF))
    out[...] = back[...].astype(BF).reshape(64, 16, 128)
    for copy in copies[1:]:
        copy.wait()
    if layer == 0:
        for step, part in enumerate(picked):
            pick("wait", (received,) + columns, step, part, sems.at[1 + step])


def pick(act, values, step, to, sem):
    index = lax.axis_index("segment")
    for layer, value in enumerate(values):
        if value is not None:
            @pl.when((index + step) % 4 == layer)
            def _():
                getattr(pltpu.make_async_copy(value, to, sem), act)()


def second_kernel(firsts_cols, own, near, far, last, out, grads, firsts_out):
    index = lax.axis_index("segment")
    for step, received in enumerate((own, near, far, last)):
        grads[...] = received[...].reshape(1024, 128).astype(F32)
        firsts_out[...] = firsts_cols[:, (index + 4 - step) % 4].reshape(1024, 128).astype(F32)
        for col in range(4):
            rows = pl.ds(col, 256, stride=4)
            part = dot_last(grads[rows, :].astype(BF), firsts_out[rows, :].astype(BF))
            out[col] = part if step == 0 else out[col] + part


def row_kernel(layer, received, upstream, held, vectors, own, left, right, across, *rest):
    slots, rest = (rest[:4], rest[4:]) if layer == 3 else (rest[0], rest[1:])
    earlier, rest = ((None,) + rest[:3], rest[3:]) if layer == 0 else ((), rest)
    outs, rest = (rest[:4], rest[4:]) if layer == 0 else (rest[:2], rest[2:])
    kept, rest = (rest[0], rest[1:]) if layer == 3 else (None, rest)
    chunks, mixed_chunks, block, mixed_block, next_chunks, weights = rest[:6]
    sems = rest[-1]
    index = lax.axis_index("segment")
    factors = (own, left, right, across)
    choose("start", factors, RING, layer, weights, sems.at[0])
    place = layer
    if layer in (3, 0):
        got, ups, mixed, inputs, vector = rest[6:11]
        pairs = [(received, got), (upstream, ups), (vectors, vector)]
        if layer == 3:
            place = 1
            pairs.append((held.at[2:4], inputs))
            for step, part in enumerate(slots):
                pairs.append((part, mixed.at[(index + 4 - step) % 4]))
        else:
            staged = rest[11]
            pairs += [(slots.at[0:1], mixed), (held.at[0:1], inputs)]
        copies = moves(pairs, sems.at[5:])
        for step in range(len(earlier)):
            pick("start", earlier, step, staged.at[step], sems.at[1 + step])
        copies[0].wait()
        received, upstream, held, vectors = got, ups, inputs, vector
    else:
        mixed = slots
    chunks[...] = received[...].reshape(1024, 128).astype(F32)
    if layer in (3, 0):
        for copy in copies[1:]:
            copy.wait()
    if layer == 3:
        write = pltpu.make_async_copy(mixed, kept, sems.at[13])
        write.start()

    def written(act, mine):
        for step in range(4):
            @pl.when(((index + step) % 4 == 0) == mine)
            def _():
                source = ups if mine else staged.at[step]
                getattr(pltpu.make_async_copy(source, outs[step], sems.at[10 + step]), act)()

    if layer == 0:
        for step in range(4):
            pick("wait", earlier, step, staged.at[step], sems.at[1 + step])
        written("start", False)
    mixed_chunks[...] = mixed[layer if layer else 0].reshape(1024, 128).astype(F32)
    choose("wait", factors, RING, layer, weights, sems.at[0])
    for row in range(4):
        rows = slice(row * 256, (row + 1) * 256)
        collect(chunks, block, row)
        collect(mixed_chunks, mixed_block, row)
        through = dot_first(weights[row], block[...].astype(BF))
        up = upstream[rows, :].astype(F32)
        gate, scale = gated(held, place, vectors, layer, rows)
        slope = (up * gate * (1.0 - gate)).astype(BF).astype(F32)
        gate_grad = (slope * mixed_block[...]).astype(BF).astype(F32)
        result = (up + through + gate_grad * scale).astype(BF)
        if layer == 0:
            ups[rows, :] = result
        else:
            outs[0][rows, :] = result
            gate, _ = gated(held, place - 1, vectors, layer - 1, rows)
            block[...] = result.astype(F32) * gate
            spread(block, next_chunks, row)
    if layer > 0:
        outs[1][...] = next_chunks[...].astype(BF).reshape(64, 16, 128)
        if layer == 3:
            write.wait()
    else:
        written("start", True)
        written("wait", True)
        written("wait", False)


def middle_kernel(layer, received, upstream, held, vectors, mixed, own, left, right, across, *rest):
    row_kernel(layer, received, upstream, held, vectors, own, left, right, across, mixed, *rest)


def final_kernel(own, near, far, last, out, sems):
    index = lax.axis_index("segment")
    pairs = []
    for step, value in enumerate((own, near, far, last)):
        lanes = pl.ds(pl.multiple_of(((index + 4 - step) % 4) * 128, 128), 128)
        pairs.append((value, out.at[:, lanes]))
    for copy in moves(pairs, sems):
        copy.wait()


IN_VMEM = pl.BlockSpec(memory_space=pltpu.VMEM)
ANYWHERE = pl.BlockSpec(memory_space=pl.ANY)


def call(kernel, count, out_shapes, scratch, flops, anywhere=0, copies=0, grant=VMEM_LIMIT, free=()):
    outs = [jax.ShapeDtypeStruct(s, d) for s, d in out_shapes]
    single = len(outs) == 1
    specs = [ANYWHERE if i in free else IN_VMEM for i in range(len(outs))]
    return pl.pallas_call(
        kernel,
        in_specs=[IN_VMEM] * (count - anywhere) + [ANYWHERE] * anywhere,
        out_shape=outs[0] if single else outs,
        out_specs=specs[0] if single else specs,
        scratch_shapes=[pltpu.VMEM(*s) if isinstance(s[0], tuple) else pltpu.VMEM(s, F32) for s in scratch]
        + ([pltpu.SemaphoreType.DMA((copies,))] if copies else []),
        compiler_params=pltpu.CompilerParams(vmem_limit_bytes=grant),
        cost_estimate=pl.CostEstimate(flops=flops, bytes_accessed=2 << 20, transcendentals=0),
    )


RING = (0, 3, 1, 2)
TALL = (1024, 128)
CHUNKS = (64, 16, 128)
BLOCK = (256, 128)
FLOPS = 2 * 4 * 256 * 256 * 128


FACTOR = ((4, 256, 256), BF)


def passed(value, step):
    return lax.ppermute(value, "segment", [(i, (i + step) % 4) for i in range(4)])


def exchanged(parts):
    return [parts[0]] + [passed(parts[step], step) for step in (1, 2, 3)]


def body(layer_inputs, first_blocks, second_blocks, gate_scale, gate_shift, top_grads):
    firsts, seconds = first_blocks[0], second_blocks[0]
    made = call(
        parts_kernel,
        4,
        [((1040, 128), BF)] * 4 + [(TALL, BF)],
        [(2, 512), (16, 128)],
        1 << 20,
        anywhere=4,
        copies=7,
        grant=LARGE_LIMIT,
    )(layer_inputs[0], gate_scale, gate_shift, top_grads)
    parts, upstream = exchanged(made[:4]), made[4]
    firsts_out = call(
        first_kernel,
        2,
        [((64, 4, 16, 128), BF)],
        [BLOCK, TALL, FACTOR, ((4, 256, 512), BF), ((4, 64, 16, 128), BF)],
        4 * FLOPS,
        anywhere=2,
        copies=6,
        free=(0,),
        grant=LARGE_LIMIT,
    )(firsts, layer_inputs[0].reshape(4, 256, 512))
    firsts_cols = lax.all_to_all(firsts_out, "seq", 0, 0, tiled=True)
    right = passed(seconds, 3)
    firsts_cols, parts, firsts, seconds, right = lax.optimization_barrier(
        (firsts_cols, parts, firsts, seconds, right)
    )
    payload, held, vectors = call(
        gate_kernel,
        7,
        [((64, 5, 16, 128), BF), ((4, 1024, 128), BF), ((4, 2, 128), F32)],
        [BLOCK, TALL, TALL, TALL, FACTOR, ((64, 4, 16, 128), BF), (TALL, BF), ((4, 16, 128), BF)],
        4 * FLOPS,
        anywhere=7,
        copies=11,
        grant=LARGE_LIMIT,
    )(seconds, firsts_cols, upstream, *parts)
    columns = [None] * 4
    columns[3] = lax.all_to_all(payload, "seq", 0, 0, tiled=True)
    seconds_all = [seconds, passed(seconds, 1), right, passed(right, 3)]
    firsts_all = [firsts, passed(firsts, 1), passed(firsts, 3)]
    columns[3], firsts_all, seconds_all = lax.optimization_barrier((columns[3], firsts_all, seconds_all))

    results, mixed = [None] * 4, None
    for l in (3, 2, 1, 0):
        grant = LARGE_LIMIT if l in (3, 0) else VMEM_LIMIT
        if l < 3:
            columns[l] = lax.all_to_all(sends, "seq", 0, 0, tiled=True)
        operands = [columns[l], *seconds_all] + (columns[1:] if l == 0 else [])
        made = call(
            functools.partial(column_kernel, l),
            len(operands),
            [(CHUNKS, BF)] * (5 if l in (3, 0) else 1),
            [TALL, TALL, FACTOR, (CHUNKS, BF)],
            FLOPS,
            anywhere=len(operands),
            copies=6,
            grant=LARGE_LIMIT if l == 3 else VMEM_LIMIT,
        )(*operands)
        back = made[0] if l in (3, 0) else made
        received = lax.all_to_all(back, "seq", 0, 0, tiled=True)
        if l == 3:
            mixed = exchanged(made[1:])
            firsts_all.append(passed(firsts_all[2], 3))
        if l == 0:
            grads = exchanged(made[1:])
        operands = [received, upstream, held, vectors, *firsts_all]
        operands += (mixed if l == 3 else [mixed]) + (results[1:] if l == 0 else [])
        outs = [(TALL, BF), (CHUNKS, BF)] if l > 0 else [(TALL, BF)] * 4
        scratch = [TALL, TALL, BLOCK, BLOCK, TALL, FACTOR]
        if l in (3, 0):
            scratch += [(CHUNKS, BF), (TALL, BF)]
        if l == 3:
            outs += [((4,) + CHUNKS, BF)]
            scratch += [((4,) + CHUNKS, BF), ((2, 1024, 128), BF), (4, 2, 128)]
        if l == 0:
            scratch += [((1,) + CHUNKS, BF), ((1, 1024, 128), BF), (4, 2, 128), ((4, 1024, 128), BF)]
        order = [0, 1, 2, 3] + [8] * (l in (2, 1)) + [4, 5, 6, 7] + list(range(8 + (l in (2, 1)), len(operands)))
        made = call(
            functools.partial(row_kernel, l) if l in (3, 0) else functools.partial(middle_kernel, l),
            len(operands),
            outs,
            scratch,
            FLOPS,
            anywhere=len(operands) if l in (3, 0) else 4,
            copies=14,
            grant=grant,
            free={3: (2,), 0: (0, 1, 2, 3)}.get(l, ()),
        )(*[operands[i] for i in order])
        if l == 3:
            made, mixed = made[:2], made[2]
        if l > 0:
            upstream, sends = made
            results[l] = upstream

    second = call(second_kernel, 5, [((4, 256, 256), F32)], [TALL, TALL], 4 * FLOPS)(firsts_cols, *grads)
    grads_out = call(final_kernel, 4, [((1024, 512), BF)], [], 1 << 20, copies=4, free=(0,))(*exchanged(made))
    return grads_out[None], second[None]


def solution(mesh):
    placed = (
        P("segment", "seq", None),
        P("segment", "seq", None, None),
        P("segment", "seq", None, None),
        P("segment", None),
        P("segment", None),
        P("seq", None),
    )
    return jax.shard_map(
        body,
        mesh=mesh,
        in_specs=placed,
        out_specs=(P("segment", "seq", None), P("segment", "seq", None, None)),
        check_vma=False,
    )
```

```python
import functools

import jax
import jax.numpy as jnp
from jax import lax
from jax.experimental import pallas as pl
from jax.experimental.pallas import tpu as pltpu
from jax.sharding import PartitionSpec as P

BF = jnp.bfloat16
F32 = jnp.float32
VMEM_LIMIT = 4 * 1024 * 1024
LARGE_LIMIT = 58 * 1024 * 1024


def dot(a, b):
    return lax.dot_general(a, b, (((1,), (0,)), ((), ())), preferred_element_type=F32)


def dot_first(a, b):
    return lax.dot_general(a, b, (((0,), (0,)), ((), ())), preferred_element_type=F32)


def dot_last(a, b):
    return lax.dot_general(a, b, (((1,), (1,)), ((), ())), preferred_element_type=F32)


def spread(block, chunks, row):
    for col in range(4):
        chunks[pl.ds(row * 4 + col, 64, stride=16), :] = block[pl.ds(col, 64, stride=4), :]


def collect(chunks, block, row):
    for col in range(4):
        block[pl.ds(col, 64, stride=4), :] = chunks[pl.ds(row * 4 + col, 64, stride=16), :]


def moves(pairs, sems):
    copies = [pltpu.make_async_copy(source, to, sems.at[i]) for i, (source, to) in enumerate(pairs)]
    for copy in copies:
        copy.start()
    return copies


def choose(act, refs, offsets, layer, to, sem):
    index = lax.axis_index("segment")
    for ref, offset in zip(refs, offsets):
        @pl.when((index + offset) % 4 == layer)
        def _():
            getattr(pltpu.make_async_copy(ref, to, sem), act)()


def parts_kernel(inputs, scale, shift, tops, *refs):
    outs, upstream, both, vectors, sems = refs[:4], refs[4], refs[5], refs[6], refs[7]
    index = lax.axis_index("segment")
    lanes = [pl.ds(pl.multiple_of(((index + step) % 4) * 128, 128), 128) for step in range(4)]
    pairs = [(scale, both.at[0:1, :]), (shift, both.at[1:2, :]), (tops.at[:, lanes[0]], upstream)]
    pairs += [(inputs.at[:, lanes[step]], outs[step].at[:1024, :]) for step in range(4)]
    copies = moves(pairs, sems)
    copies[0].wait()
    copies[1].wait()
    vectors[...] = jnp.zeros_like(vectors)
    for step in range(4):
        for place in range(2):
            left = both[place:place + 1, lanes[step]]
            for term in range(3):
                piece = left.astype(BF).astype(F32)
                vectors[place * 3 + term:place * 3 + term + 1, :] = piece
                left = left - piece
        outs[step][1024:, :] = vectors[...].astype(BF)
    for copy in copies[2:]:
        copy.wait()


def first_kernel(firsts, inputs, out, block, chunks, weights, held, done, sems):
    copies = moves([(firsts, weights), (inputs, held)], sems)
    for copy in copies:
        copy.wait()
    written = []
    for part in range(4):
        lanes = slice(part * 128, (part + 1) * 128)
        for row in range(4):
            block[...] = dot(weights[row], held[row, :, lanes])
            spread(block, chunks, row)
        done[part] = chunks[...].astype(BF).reshape(64, 16, 128)
        written.append(pltpu.make_async_copy(done.at[part], out.at[:, part], sems.at[2 + part]))
        written[-1].start()
    for copy in written:
        copy.wait()


def gated(inputs, place, vectors, layer, rows):
    scale, shift = vectors[layer, 0:1, :], vectors[layer, 1:2, :]
    return jax.nn.sigmoid(inputs[place, rows, :].astype(F32) * scale + shift), scale


def gate_kernel(seconds, firsts_cols, upstream, own, near, far, last, out, held, vectors, *scratch):
    block, chunks, wide, mixed, weights, fcols, ups, terms, sems = scratch
    index = lax.axis_index("segment")
    pairs = [(seconds, weights), (firsts_cols, fcols), (upstream, ups)]
    for step, part in enumerate((own, near, far, last)):
        layer = (index + 4 - step) % 4
        pairs += [(part.at[:1024, :], held.at[layer]), (part.at[1024:, :], terms.at[layer])]
    copies = moves(pairs, sems)
    copies[0].wait()
    copies[1].wait()
    for part in range(4):
        wide[...] = fcols[:, part].reshape(1024, 128).astype(F32)
        for col in range(4):
            rows = pl.ds(col, 256, stride=4)
            mixed[rows, :] = dot(weights[col], wide[rows, :].astype(BF))
        out[:, part] = mixed[...].astype(BF).reshape(64, 16, 128)
    for copy in copies[2:]:
        copy.wait()
    for layer in range(4):
        values = terms[layer].astype(F32)
        vectors[layer, 0:1, :] = values[0:1, :] + (values[1:2, :] + values[2:3, :])
        vectors[layer, 1:2, :] = values[3:4, :] + (values[4:5, :] + values[5:6, :])
    for row in range(4):
        rows = slice(row * 256, (row + 1) * 256)
        gate, _ = gated(held, 3, vectors, 3, rows)
        block[...] = ups[rows, :].astype(F32) * gate
        spread(block, chunks, row)
    out[:, 4] = chunks[...].astype(BF).reshape(64, 16, 128)


def column_kernel(layer, received, own, left, right, across, *rest):
    columns, rest = (rest[:3], rest[3:]) if layer == 0 else ((), rest)
    if layer == 0:
        columns = columns[:2] + (columns[2].at[:, 4],)
    out, (grads, back, weights, got, sems) = rest[0], rest[-5:]
    picked = rest[1:-5]
    index = lax.axis_index("segment")
    factors = (own, left, right, across)
    choose("start", factors, RING, layer, weights, sems.at[5])
    pairs = [(received.at[:, 4] if layer == 3 else received, got)]
    if layer == 3:
        pairs += [(received.at[:, (index + step) % 4], part) for step, part in enumerate(picked)]
    copies = moves(pairs, sems)
    if layer == 0:
        for step, part in enumerate(picked):
            pick("start", (received,) + columns, step, part, sems.at[1 + step])
    copies[0].wait()
    grads[...] = got[...].reshape(1024, 128).astype(F32)
    choose("wait", factors, RING, layer, weights, sems.at[5])
    for col in range(4):
        rows = pl.ds(col, 256, stride=4)
        back[rows, :] = dot_first(weights[col], grads[rows, :].astype(BF))
    out[...] = back[...].astype(BF).reshape(64, 16, 128)
    for copy in copies[1:]:
        copy.wait()
    if layer == 0:
        for step, part in enumerate(picked):
            pick("wait", (received,) + columns, step, part, sems.at[1 + step])


def pick(act, values, step, to, sem):
    index = lax.axis_index("segment")
    for layer, value in enumerate(values):
        if value is not None:
            @pl.when((index + step) % 4 == layer)
            def _():
                getattr(pltpu.make_async_copy(value, to, sem), act)()


def second_kernel(firsts_cols, own, near, far, last, out, grads, firsts_out):
    index = lax.axis_index("segment")
    for step, received in enumerate((own, near, far, last)):
        grads[...] = received[...].reshape(1024, 128).astype(F32)
        firsts_out[...] = firsts_cols[:, (index + 4 - step) % 4].reshape(1024, 128).astype(F32)
        for col in range(4):
            rows = pl.ds(col, 256, stride=4)
            part = dot_last(grads[rows, :].astype(BF), firsts_out[rows, :].astype(BF))
            out[col] = part if step == 0 else out[col] + part


def row_kernel(layer, received, upstream, held, vectors, own, left, right, across, *rest):
    slots, rest = (rest[:4], rest[4:]) if layer == 3 else (rest[0], rest[1:])
    earlier, rest = ((None,) + rest[:3], rest[3:]) if layer == 0 else ((), rest)
    outs, rest = (rest[:4], rest[4:]) if layer == 0 else (rest[:2], rest[2:])
    kept, rest = (rest[0], rest[1:]) if layer == 3 else (None, rest)
    chunks, mixed_chunks, block, mixed_block, next_chunks, weights = rest[:6]
    sems = rest[-1]
    index = lax.axis_index("segment")
    factors = (own, left, right, across)
    choose("start", factors, RING, layer, weights, sems.at[0])
    place = layer
    if layer in (3, 0):
        got, ups, mixed, inputs, vector = rest[6:11]
        pairs = [(received, got), (upstream, ups), (vectors, vector)]
        if layer == 3:
            place = 1
            pairs.append((held.at[2:4], inputs))
            for step, part in enumerate(slots):
                pairs.append((part, mixed.at[(index + 4 - step) % 4]))
        else:
            staged = rest[11]
            pairs += [(slots.at[0:1], mixed), (held.at[0:1], inputs)]
        copies = moves(pairs, sems.at[5:])
        for step in range(len(earlier)):
            pick("start", earlier, step, staged.at[step], sems.at[1 + step])
        copies[0].wait()
        received, upstream, held, vectors = got, ups, inputs, vector
    else:
        mixed = slots
    chunks[...] = received[...].reshape(1024, 128).astype(F32)
    if layer in (3, 0):
        for copy in copies[1:]:
            copy.wait()
    if layer == 3:
        write = pltpu.make_async_copy(mixed, kept, sems.at[13])
        write.start()

    def written(act, mine):
        for step in range(4):
            @pl.when(((index + step) % 4 == 0) == mine)
            def _():
                source = ups if mine else staged.at[step]
                getattr(pltpu.make_async_copy(source, outs[step], sems.at[10 + step]), act)()

    if layer == 0:
        for step in range(4):
            pick("wait", earlier, step, staged.at[step], sems.at[1 + step])
        written("start", False)
    mixed_chunks[...] = mixed[layer if layer else 0].reshape(1024, 128).astype(F32)
    choose("wait", factors, RING, layer, weights, sems.at[0])
    for row in range(4):
        rows = slice(row * 256, (row + 1) * 256)
        collect(chunks, block, row)
        collect(mixed_chunks, mixed_block, row)
        through = dot_first(weights[row], block[...].astype(BF))
        up = upstream[rows, :].astype(F32)
        gate, scale = gated(held, place, vectors, layer, rows)
        slope = (up * gate * (1.0 - gate)).astype(BF).astype(F32)
        gate_grad = (slope * mixed_block[...]).astype(BF).astype(F32)
        result = (up + through + gate_grad * scale).astype(BF)
        if layer == 0:
            ups[rows, :] = result
        else:
            outs[0][rows, :] = result
            gate, _ = gated(held, place - 1, vectors, layer - 1, rows)
            block[...] = result.astype(F32) * gate
            spread(block, next_chunks, row)
    if layer > 0:
        outs[1][...] = next_chunks[...].astype(BF).reshape(64, 16, 128)
        if layer == 3:
            write.wait()
    else:
        written("start", True)
        written("wait", True)
        written("wait", False)


def middle_kernel(layer, received, upstream, held, vectors, mixed, own, left, right, across, *rest):
    row_kernel(layer, received, upstream, held, vectors, own, left, right, across, mixed, *rest)


def final_kernel(own, near, far, last, out, sems):
    index = lax.axis_index("segment")
    pairs = []
    for step, value in enumerate((own, near, far, last)):
        lanes = pl.ds(pl.multiple_of(((index + 4 - step) % 4) * 128, 128), 128)
        pairs.append((value, out.at[:, lanes]))
    for copy in moves(pairs, sems):
        copy.wait()


IN_VMEM = pl.BlockSpec(memory_space=pltpu.VMEM)
ANYWHERE = pl.BlockSpec(memory_space=pl.ANY)


def call(kernel, count, out_shapes, scratch, flops, anywhere=0, copies=0, grant=VMEM_LIMIT, free=()):
    outs = [jax.ShapeDtypeStruct(s, d) for s, d in out_shapes]
    single = len(outs) == 1
    specs = [ANYWHERE if i in free else IN_VMEM for i in range(len(outs))]
    return pl.pallas_call(
        kernel,
        in_specs=[IN_VMEM] * (count - anywhere) + [ANYWHERE] * anywhere,
        out_shape=outs[0] if single else outs,
        out_specs=specs[0] if single else specs,
        scratch_shapes=[pltpu.VMEM(*s) if isinstance(s[0], tuple) else pltpu.VMEM(s, F32) for s in scratch]
        + ([pltpu.SemaphoreType.DMA((copies,))] if copies else []),
        compiler_params=pltpu.CompilerParams(vmem_limit_bytes=grant),
        cost_estimate=pl.CostEstimate(flops=flops, bytes_accessed=2 << 20, transcendentals=0),
    )


RING = (0, 3, 1, 2)
TALL = (1024, 128)
CHUNKS = (64, 16, 128)
BLOCK = (256, 128)
FLOPS = 2 * 4 * 256 * 256 * 128


FACTOR = ((4, 256, 256), BF)


def passed(value, step):
    return lax.ppermute(value, "segment", [(i, (i + step) % 4) for i in range(4)])


def exchanged(parts):
    return [parts[0]] + [passed(parts[step], step) for step in (1, 2, 3)]


def body(layer_inputs, first_blocks, second_blocks, gate_scale, gate_shift, top_grads):
    firsts, seconds = first_blocks[0], second_blocks[0]
    made = call(
        parts_kernel,
        4,
        [((1040, 128), BF)] * 4 + [(TALL, BF)],
        [(2, 512), (16, 128)],
        1 << 20,
        anywhere=4,
        copies=7,
        grant=LARGE_LIMIT,
    )(layer_inputs[0], gate_scale, gate_shift, top_grads)
    parts, upstream = exchanged(made[:4]), made[4]
    firsts_out = call(
        first_kernel,
        2,
        [((64, 4, 16, 128), BF)],
        [BLOCK, TALL, FACTOR, ((4, 256, 512), BF), ((4, 64, 16, 128), BF)],
        4 * FLOPS,
        anywhere=2,
        copies=6,
        free=(0,),
        grant=LARGE_LIMIT,
    )(firsts, layer_inputs[0].reshape(4, 256, 512))
    firsts_cols = lax.all_to_all(firsts_out, "seq", 0, 0, tiled=True)
    right = passed(seconds, 3)
    firsts_cols, parts, firsts, seconds, right = lax.optimization_barrier(
        (firsts_cols, parts, firsts, seconds, right)
    )
    payload, held, vectors = call(
        gate_kernel,
        7,
        [((64, 5, 16, 128), BF), ((4, 1024, 128), BF), ((4, 2, 128), F32)],
        [BLOCK, TALL, TALL, TALL, FACTOR, ((64, 4, 16, 128), BF), (TALL, BF), ((4, 16, 128), BF)],
        4 * FLOPS,
        anywhere=7,
        copies=11,
        grant=LARGE_LIMIT,
    )(seconds, firsts_cols, upstream, *parts)
    columns = [None] * 4
    columns[3] = lax.all_to_all(payload, "seq", 0, 0, tiled=True)
    seconds_all = [seconds, passed(seconds, 1), right, passed(right, 3)]
    firsts_all = [firsts, passed(firsts, 1), passed(firsts, 3)]
    columns[3], firsts_all, seconds_all = lax.optimization_barrier((columns[3], firsts_all, seconds_all))

    results, mixed = [None] * 4, None
    for l in (3, 2, 1, 0):
        grant = LARGE_LIMIT if l in (3, 0) else VMEM_LIMIT
        if l < 3:
            columns[l] = lax.all_to_all(sends, "seq", 0, 0, tiled=True)
        operands = [columns[l], *seconds_all] + (columns[1:] if l == 0 else [])
        made = call(
            functools.partial(column_kernel, l),
            len(operands),
            [(CHUNKS, BF)] * (5 if l in (3, 0) else 1),
            [TALL, TALL, FACTOR, (CHUNKS, BF)],
            FLOPS,
            anywhere=len(operands),
            copies=6,
            grant=LARGE_LIMIT if l == 3 else VMEM_LIMIT,
        )(*operands)
        back = made[0] if l in (3, 0) else made
        received = lax.all_to_all(back, "seq", 0, 0, tiled=True)
        if l == 3:
            mixed = exchanged(made[1:])
            firsts_all.append(passed(firsts_all[2], 3))
        if l == 0:
            grads = exchanged(made[1:])
        operands = [received, upstream, held, vectors, *firsts_all]
        operands += (mixed if l == 3 else [mixed]) + (results[1:] if l == 0 else [])
        outs = [(TALL, BF), (CHUNKS, BF)] if l > 0 else [(TALL, BF)] * 4
        scratch = [TALL, TALL, BLOCK, BLOCK, TALL, FACTOR]
        if l in (3, 0):
            scratch += [(CHUNKS, BF), (TALL, BF)]
        if l == 3:
            outs += [((4,) + CHUNKS, BF)]
            scratch += [((4,) + CHUNKS, BF), ((2, 1024, 128), BF), (4, 2, 128)]
        if l == 0:
            scratch += [((1,) + CHUNKS, BF), ((1, 1024, 128), BF), (4, 2, 128), ((4, 1024, 128), BF)]
        order = [0, 1, 2, 3] + [8] * (l in (2, 1)) + [4, 5, 6, 7] + list(range(8 + (l in (2, 1)), len(operands)))
        made = call(
            functools.partial(row_kernel, l) if l in (3, 0) else functools.partial(middle_kernel, l),
            len(operands),
            outs,
            scratch,
            FLOPS,
            anywhere=len(operands) if l in (3, 0) else 4,
            copies=14,
            grant=grant,
            free={3: (2,), 0: (0, 1, 2, 3)}.get(l, ()),
        )(*[operands[i] for i in order])
        if l == 3:
            made, mixed = made[:2], made[2]
        if l > 0:
            upstream, sends = made
            results[l] = upstream

    second = call(second_kernel, 5, [((4, 256, 256), F32)], [TALL, TALL], 4 * FLOPS)(firsts_cols, *grads)
    grads_out = call(final_kernel, 4, [((1024, 512), BF)], [], 1 << 20, copies=4, free=(0,))(*exchanged(made))
    return grads_out[None], second[None]


def solution(mesh):
    placed = (
        P("segment", "seq", None),
        P("segment", "seq", None, None),
        P("segment", "seq", None, None),
        P("segment", None),
        P("segment", None),
        P("seq", None),
    )
    return jax.shard_map(
        body,
        mesh=mesh,
        in_specs=placed,
        out_specs=(P("segment", "seq", None), P("segment", "seq", None, None)),
        check_vma=False,
    )
```
